128 devices in a mesh: tm: 4 (over x_hi, core), space: 32 (over y, x_lo, z).
Axes of the slice: x: 4 (x_hi: 2, x_lo: 2; x = x_hi * 2 + x_lo), y: 4, z: 4, core: 2. Of those that a mesh axis runs over, the one named last changes fastest.
Arguments:
- states: float32 [8, 3, 128, 128, 128], P('tm', None, 'space'), may hold values from -6 to 6
- sources: float32 [8, 3, 128, 128, 128], P('tm', None, 'space'), may hold values from -6 to 6
- conductivity: float32 [128, 128, 128], P('space'), may hold values from 0.5 to 4
- gap_tile: int32 [8, 4096, 1], P('tm', 'space'), may hold values from 0 to 31; in each aligned block of 128 rows (0 to 127, 128 to 255, ..., all dimensions but the last counted through in order) at most 8 rows name the same one
- gap_row: int32 [8, 4096], P('tm', 'space'), may hold values from 0 to 127
Outputs:
- new_states: float32 [8, 3, 128, 128, 128], P('tm', None, 'space')
The draws below stay inside these ranges and needn't reach their ends.
Inputs may be any that keep to these rules, and one draw needn't show every extreme that they name: `gap_tile`: in each slice no tile maps more than 8 of its own 128 interface rows to any one tile.
All inputs are finite; a program needn't handle non-finite values.
Results may differ from the reference program's by a relative error of at most 0.0001.
Values sent between devices are 32-bit elements; how exact they have to be, the bound alone decides.
A program may use at most 128 MiB of HBM per device.

```python
import math
import jax
import jax.numpy as jnp
import numpy as np

CX = 4
CY = 128
CZ = 128
STEPS = 4
SWEEPS = 3
COARSE_SWEEPS = 3
SLICES = 8
NX = 128
CAP = 8
N_SPACE = 32


def place_ends(values, key, low, top_value):
    place = [jax.random.randint(jax.random.fold_in(key, axis), (), 0, length) for axis, length in enumerate(values.shape)]
    widest = values.shape.index(max(values.shape))
    beside = place[:widest] + [(place[widest] + 1) % values.shape[widest]] + place[widest + 1:]
    return values.at[tuple(place)].set(low).at[tuple(beside)].set(top_value)


def level_of(key, dims, split, least, high):
    def one(position, blocks):
        draws = jax.random.uniform(jax.random.fold_in(jax.random.fold_in(key, 6), position), (blocks,), jnp.float32, least / len(split), high / len(split))
        return jnp.repeat(jnp.exp(draws), dims[position] // blocks).reshape((-1,) + (1,) * (len(dims) - position - 1))

    gain = one(*split[0])
    for cut in split[1:]:
        gain = gain * one(*cut)
    return gain


def assign_block(rng, own, number, rows, number_of, top, most, skew):
    ranking = jax.random.permutation(rng, number_of)
    packed, usual = shares(number_of, rows * top, most, skew, True), shares(number_of, rows * top, most, skew, False)
    places = jnp.arange(number_of)

    def named(lengths, offset_by):
        used = int((lengths > 0).sum())
        fixed = max(1, used // 4)
        passed = fixed + (places - fixed + offset_by * (used - fixed)) % max(1, number_of - fixed)
        return jnp.zeros((number_of,), jnp.int32).at[ranking[jnp.where(places < fixed, places, passed)]].set(jnp.asarray(lengths, jnp.int32))

    lengths = jnp.where(number % 4 == 0, named(packed, number // 4), named(usual, number - number // 4 - 1))
    mixed = jax.random.permutation(jax.random.fold_in(own, 3), number_of)
    source_of, taker = mixed[0:number_of // 2 * 2:2], mixed[1:number_of // 2 * 2:2]
    room = jnp.minimum(lengths[source_of] - 1, most - lengths[taker]) // 2
    room = jnp.where((source_of == ranking[0]) | (taker == ranking[0]) | (lengths[taker] == 0), 0, jnp.maximum(room, 0))
    passed = jax.random.randint(jax.random.fold_in(own, 4), (number_of // 2,), 0, 1 << 20) % (room + 1)
    lengths = lengths.at[source_of].add(-passed).at[taker].add(passed)
    items = jnp.searchsorted(jnp.cumsum(lengths), jnp.arange(rows * top), side="right").astype(jnp.int32)
    grid = items.reshape(top, rows).T
    grid = grid[jax.random.permutation(jax.random.fold_in(own, 1), rows)]
    offset_by = jax.random.randint(jax.random.fold_in(own, 2), (rows, 1), 0, top)
    return jnp.take_along_axis(grid, (jnp.arange(top)[None, :] + offset_by) % top, axis=1)


def shares(count, total, limit, slope, full):
    portions = [(1 << 20) // math.isqrt(grade ** slope) + 1 for grade in range(1, count + 1)]
    largest = limit if full else min(limit, max(-(-total // count), total * portions[0] // sum(portions)))
    least = 1 if total - largest >= count - 1 else 0
    given, spare = [largest] + [least] * (count - 1), total - largest - least * (count - 1)
    while spare > 0:
        free = [i for i in range(1, count) if given[i] < largest] or [i for i in range(1, count) if given[i] < limit]
        whole, remaining = sum([portions[i] for i in free]), spare
        for i in free:
            more = min(limit - given[i], max(1, remaining * portions[i] // whole), spare)
            given[i] = given[i] + more
            spare = spare - more
    return np.array(given)


def noise(own_key, extent, scale, bound, pieces=(), dtype=jnp.bfloat16):
    array = scale * jax.random.normal(own_key, extent, jnp.float32)
    if pieces:
        array = array * level_of(own_key, extent, pieces, -0.22, 0.18)
    return jnp.clip(array, -bound, bound).astype(dtype)


def setup_inputs(seed: int = 0) -> dict:
    arg_keys = jax.random.split(jax.random.key(seed), 6)
    states = noise(arg_keys[0], (SLICES, 3, NX, CY, CZ), 1.0, 6.0, ((0, 4), (2, 32)), jnp.float32)
    sources = noise(arg_keys[1], (SLICES, 3, NX, CY, CZ), 1.0, 6.0, ((0, 4), (2, 32)), jnp.float32)
    conductivity = jnp.clip(jnp.exp(math.log(4.0) - 2.0794415 * jax.random.uniform(arg_keys[2], (NX, CY, CZ), jnp.float32) ** level_of(arg_keys[2], (NX, CY, CZ), ((0, 32),), -0.2, 0.2)), 0.5, 4.0)
    gap_tile_keys = jax.random.split(jax.random.fold_in(arg_keys[3], 1), SLICES * (N_SPACE * CY) // CY)
    gap_tile_turns = jax.random.permutation(jax.random.fold_in(arg_keys[3], 3), SLICES * (N_SPACE * CY) // CY)
    gap_tile = jax.vmap(lambda own, number: assign_block(jax.random.fold_in(arg_keys[3], 2), own, number, CY, N_SPACE, 1, CAP, 2))(gap_tile_keys, gap_tile_turns).reshape((SLICES, N_SPACE * CY, 1))
    gap_row = place_ends(jax.random.randint(arg_keys[4], (SLICES, N_SPACE * CY), 0, CY), jax.random.fold_in(arg_keys[4], 1), 0, CY - 1).astype(jnp.int32)
    return dict(states=states, sources=sources, conductivity=conductivity, gap_tile=gap_tile, gap_row=gap_row)


inverse_step = 2.0
gap_gain = 1.0


def neighbours(field):
    padded = jnp.pad(field, ((0, 0), (1, 1), (1, 1), (1, 1)))
    total = padded[:, 2:, 1:-1, 1:-1] + padded[:, :-2, 1:-1, 1:-1]
    total = total + padded[:, 1:-1, 2:, 1:-1] + padded[:, 1:-1, :-2, 1:-1]
    total = total + padded[:, 1:-1, 1:-1, 2:] + padded[:, 1:-1, 1:-1, :-2]
    return total


def jacobi(field, rhs, diag, sweeps):
    for sweep in range(sweeps):
        field = (rhs + neighbours(field)) / diag
    return field


def fine(field, source, conduct, tiles, rows_dst):
    rate = inverse_step * conduct
    dest = (tiles * CY + rows_dst).astype(jnp.int32)
    for step in range(STEPS):
        rows = field[0, ::CX].reshape(N_SPACE * CY, CZ)
        coupled = jax.ops.segment_sum(rows, dest, num_segments=N_SPACE * CY).reshape(N_SPACE, CY, CZ)
        rhs = rate * field + source
        rhs = rhs.at[0, ::CX].add(gap_gain * coupled)
        field = jacobi(field, rhs, rate + 6.0, SWEEPS)
    return field


def coarse(field, source, conduct):
    rate = inverse_step * conduct / STEPS
    return jacobi(field, rate * field + source, rate + 6.0, COARSE_SWEEPS)


def reference(states, sources, conductivity, gap_tile, gap_row):
    ends = []
    jumps = []
    for slot in range(SLICES):
        end = fine(states[slot], sources[slot], conductivity, gap_tile[slot, :, 0], gap_row[slot])
        ends.append(end)
        jumps.append(end - coarse(states[slot], sources[slot], conductivity))
    result = [ends[SLICES - 1]]
    for slot in range(SLICES - 1):
        result.append(coarse(result[slot], sources[slot], conductivity) + jumps[slot])
    return jnp.stack(result)
```

```python
import jax
import jax.numpy as jnp
from jax import lax
from jax.experimental import pallas as pl
from jax.experimental.pallas import tpu as pltpu
from jax.sharding import PartitionSpec as P

STEPS = 4
SWEEPS = 3
CAP = 8
PAD = 8

INVERSE_STEP = 2.0
GAP_GAIN = 1.0
MESH = pl.DeviceIdType.MESH
HIGHEST = lax.Precision.HIGHEST


def kernel(
    n_space, n_tm,
    states, sources, conduct, gap_tile, gap_row,
    out,
    v, rhs, sig, alpha, dinv, w1, w2, delta, cond8, gamma, dinv_c, new0, passed,
    pick, place, packed, landed, names, names_in, coupled,
    halo_send, halo_recv, gap_send, gap_recv, name_send, name_recv,
    cond_send, cond_recv, delta_send, delta_recv, pass_send, pass_recv,
):
    me = lax.axis_index("space")
    rank = lax.axis_index("tm")
    n_slice, n_comp, planes, rows, width = states.shape
    slots = n_space * CAP
    inner = pl.ds(PAD, rows)
    left_dev = {"space": jnp.maximum(me - 1, 0)}
    right_dev = {"space": jnp.minimum(me + 1, n_space - 1)}
    has_left = me > 0
    has_right = me < n_space - 1
    lane = lax.broadcasted_iota(jnp.int32, (rows, width), 1)
    sub = lax.broadcasted_iota(jnp.int32, (rows, width), 0)

    edge_rows = jnp.zeros((PAD, width), jnp.float32)
    no_plane = jnp.zeros((rows, width), jnp.float32)

    def pad_planes(ref, index, count):
        for p in range(count):
            ref[index + (p, pl.ds(0, PAD))] = edge_rows
            ref[index + (p, pl.ds(PAD + rows, PAD))] = edge_rows

    def pad_fields(i, _):
        s, c = i // n_comp, i % n_comp
        for par in range(2):
            pad_planes(v, (par, s, c), planes + 2)
        pad_planes(delta, (s, c), planes + 6)
        for p in range(planes):
            v[0, s, c, p + 1, inner] = states[s, c, p]
        return 0

    lax.fori_loop(0, n_slice * n_comp, pad_fields, 0)
    pad_planes(w1, (), planes + 4)
    pad_planes(w2, (), planes + 2)

    def clear(first, past):
        def one(i, _):
            s, c = i // n_comp, i % n_comp
            for par in range(2):
                v[par, s, c, 0 if first else planes + 1, inner] = no_plane
            for p in range(3):
                delta[s, c, p if first else planes + 3 + p, inner] = no_plane
            return 0

        lax.fori_loop(0, n_slice * n_comp, one, 0)
        for p in range(2):
            cond8[p if first else planes + 2 + p] = no_plane

    @pl.when(jnp.logical_not(has_left))
    def _():
        clear(True, 0)

    @pl.when(jnp.logical_not(has_right))
    def _():
        clear(False, 0)

    barrier = pltpu.get_barrier_semaphore()

    def greet(i, _):
        peer = lax.rem(me + i, n_space)
        pl.semaphore_signal(barrier, inc=1, device_id={"space": peer}, device_id_type=MESH)
        return 0

    lax.fori_loop(1, n_space, greet, 0)
    next_rank = lax.rem(rank + 1, n_tm)
    for peer in (next_rank, lax.rem(rank + n_tm - 1, n_tm)):
        pl.semaphore_signal(barrier, inc=1, device_id={"tm": peer}, device_id_type=MESH)

    for p in range(planes):
        rate = INVERSE_STEP * conduct[p]
        inverse = 1.0 / (rate + 6.0)
        dinv[p] = inverse
        alpha[p] = rate * inverse
        cond8[p + 2] = conduct[p]

    def scaled(i, _):
        s, c = i // n_comp, i % n_comp
        for p in range(planes):
            sig[s, c, p] = sources[s, c, p] * dinv[p]
        return 0

    lax.fori_loop(0, n_slice * n_comp, scaled, 0)

    for s in range(n_slice):
        tile_col = jnp.broadcast_to(gap_tile[s].astype(jnp.float32), (rows, width))
        tile_row = tile_col.T
        before = jnp.where((tile_col == tile_row) & (sub < lane), 1.0, 0.0)
        position = jnp.sum(before, axis=0, keepdims=True)
        slot = tile_row[0:1] * CAP + position
        wide = lax.broadcasted_iota(jnp.int32, (slots, rows), 0).astype(jnp.float32)
        chosen = jnp.where(wide == slot, 1.0, 0.0)
        pick[s] = chosen
        target = gap_row[s:s + 1].astype(jnp.float32) + 1.0
        named = jnp.sum(chosen * target, axis=1, keepdims=True)
        names[s] = jnp.broadcast_to(named, (slots, width))

    def pack(s, gp, par):
        packed[gp, s] = jnp.dot(
            pick[s], v[par, s, 0, 1, inner], precision=HIGHEST, preferred_element_type=jnp.float32
        )

    for s in range(n_slice):
        pack(s, 0, 0)

    pl.semaphore_wait(barrier, n_space - 1 + 2)

    def halo_copy(par, s, c, way):
        return pltpu.make_async_remote_copy(
            src_ref=v.at[par, s, c, 1 if way == 0 else planes, inner],
            dst_ref=v.at[par, s, c, planes + 1 if way == 0 else 0, inner],
            send_sem=halo_send.at[par, s, c, way],
            recv_sem=halo_recv.at[par, s, c, way],
            device_id=left_dev if way == 0 else right_dev,
            device_id_type=MESH,
        )

    def delta_copy(s, c, way):
        return pltpu.make_async_remote_copy(
            src_ref=delta.at[s, c, pl.ds(3 if way == 0 else planes, 3), inner],
            dst_ref=delta.at[s, c, pl.ds(planes + 3 if way == 0 else 0, 3), inner],
            send_sem=delta_send.at[s, c, way],
            recv_sem=delta_recv.at[s, c, way],
            device_id=left_dev if way == 0 else right_dev,
            device_id_type=MESH,
        )

    def cond_copy(way):
        return pltpu.make_async_remote_copy(
            src_ref=cond8.at[pl.ds(2 if way == 0 else planes, 2)],
            dst_ref=cond8.at[pl.ds(planes + 2 if way == 0 else 0, 2)],
            send_sem=cond_send.at[way],
            recv_sem=cond_recv.at[way],
            device_id=left_dev if way == 0 else right_dev,
            device_id_type=MESH,
        )

    def start(copy):
        @pl.when(has_left)
        def _():
            copy(0).start()

        @pl.when(has_right)
        def _():
            copy(1).start()

    def arrived(copy):
        @pl.when(has_right)
        def _():
            copy(0).wait_recv()

        @pl.when(has_left)
        def _():
            copy(1).wait_recv()

    def sent(copy):
        @pl.when(has_left)
        def _():
            copy(0).wait_send()

        @pl.when(has_right)
        def _():
            copy(1).wait_send()

    def scatter(source, landing, send_sem, recv_sem):
        def one(i, _):
            peer = lax.rem(me + i, n_space)
            pltpu.make_async_remote_copy(
                src_ref=source.at[:, pl.ds(pl.multiple_of(peer * CAP, CAP), CAP)],
                dst_ref=landing.at[:, pl.ds(pl.multiple_of(me * CAP, CAP), CAP)],
                send_sem=send_sem,
                recv_sem=recv_sem,
                device_id={"space": peer},
                device_id_type=MESH,
            ).start()
            return 0

        lax.fori_loop(1, n_space, one, 0)
        own = pl.ds(pl.multiple_of(me * CAP, CAP), CAP)
        for s in range(n_slice):
            landing[s, own] = source[s, own]

    def all_of(source, landing, send_sem, recv_sem):
        most = pl.ds(0, (n_space - 1) * CAP)
        return pltpu.make_async_remote_copy(
            src_ref=source.at[:, most],
            dst_ref=landing.at[:, most],
            send_sem=send_sem,
            recv_sem=recv_sem,
            device_id=left_dev,
            device_id_type=MESH,
        )

    def gap_refs(gp):
        return packed.at[gp], landed.at[gp], gap_send.at[gp], gap_recv.at[gp]

    name_refs = (names, names_in, name_send.at[0], name_recv.at[0])
    scatter(*name_refs)
    scatter(*gap_refs(0))

    def start_all(i, _):
        s, c = i // n_comp, i % n_comp
        start(lambda way: halo_copy(0, s, c, way))
        return 0

    lax.fori_loop(0, n_slice * n_comp, start_all, 0)
    start(cond_copy)

    def beside(ref, index, p):
        here = ref[index + (p, inner)]
        total = ref[index + (p - 1, inner)] + ref[index + (p + 1, inner)]
        total = total + ref[index + (p, pl.ds(PAD - 1, rows))] + ref[index + (p, pl.ds(PAD + 1, rows))]
        total = total + jnp.where(lane == 0, 0.0, pltpu.roll(here, 1, 1))
        total = total + jnp.where(lane == width - 1, 0.0, pltpu.roll(here, width - 1, 1))
        return total, here

    def field(step, sweep, s, c, gap):
        count = step * SWEEPS + sweep
        par = lax.rem(count, 2)
        onto = 1 - par
        arrived(lambda way: halo_copy(par, s, c, way))

        @pl.when(count > 0)
        def _():
            sent(lambda way: halo_copy(onto, s, c, way))

        def plane(p):
            total, here = beside(v, (par, s, c), p)
            if sweep == 0:
                base = alpha[p - 1] * here + sig[s, c, p - 1]
                if gap and p == 1:
                    base = base + dinv[0] * coupled[s]
                rhs[s, c, p - 1] = base
            else:
                base = rhs[s, c, p - 1]
            v[onto, s, c, p, inner] = base + dinv[p - 1] * total

        plane(1)
        plane(planes)
        more = step < STEPS - 1 if sweep == SWEEPS - 1 else None

        def send():
            start(lambda way: halo_copy(onto, s, c, way))

        if more is None:
            send()
        else:
            pl.when(more)(send)
        for p in range(2, planes):
            plane(p)

    def one_step(step, _):
        gp = lax.rem(step, 2)
        for sweep in range(SWEEPS):

            def free(i, _, sweep=sweep):
                field(step, sweep, i // 2, 1 + i % 2, False)
                return 0

            lax.fori_loop(0, n_slice * 2, free, 0)
            if sweep == 0:

                @pl.when(step == 0)
                def _():
                    all_of(*name_refs).wait_recv()
                    for s in range(n_slice):
                        for part in range(2):
                            held = names_in[s, pl.ds(part * 128, 128)]
                            hit = jnp.where(held == (lane + 1).astype(jnp.float32), 1.0, 0.0)
                            place[s, :, pl.ds(part * 128, 128)] = hit.T

                all_of(*gap_refs(gp)).wait_recv()
                for s in range(n_slice):
                    coupled[s] = GAP_GAIN * jnp.dot(
                        place[s], landed[gp, s], precision=HIGHEST, preferred_element_type=jnp.float32
                    )

            def tied(s, _, sweep=sweep):
                field(step, sweep, s, 0, True)
                return 0

            lax.fori_loop(0, n_slice, tied, 0)

        @pl.when(step < STEPS - 1)
        def _():
            later = 1 - gp
            par = lax.rem((step + 1) * SWEEPS, 2)

            @pl.when(step > 0)
            def _():
                all_of(*gap_refs(later)).wait_send()

            for s in range(n_slice):
                pack(s, later, par)
            scatter(*gap_refs(later))

        return 0

    lax.fori_loop(0, STEPS, one_step, 0)
    end = (STEPS * SWEEPS) % 2

    def pass_copy(source, c):
        return pltpu.make_async_remote_copy(
            src_ref=source,
            dst_ref=new0.at[c],
            send_sem=pass_send.at[c],
            recv_sem=pass_recv.at[c],
            device_id={"tm": next_rank},
            device_id_type=MESH,
        )

    @pl.when(rank == n_tm - 1)
    def _():
        def one(c, _):
            pass_copy(v.at[end, n_slice - 1, c, pl.ds(1, planes), inner], c).start()
            return 0

        lax.fori_loop(0, n_comp, one, 0)

    arrived(cond_copy)
    for p in range(planes + 4):
        rate = INVERSE_STEP * cond8[p] / STEPS
        inverse = 1.0 / (rate + 6.0)
        if p < 2:
            inverse = jnp.where(has_left, inverse, 0.0)
        if p >= planes + 2:
            inverse = jnp.where(has_right, inverse, 0.0)
        dinv_c[p] = inverse
        gamma[p] = rate * inverse

    def coarse(s, c, p):
        total, _ = beside(w2, (), p + 1)
        return gamma[p + 2] * delta[s, c, p + 3, inner] + dinv_c[p + 2] * total

    def coarse_before(s, c):
        for p in range(planes + 4):
            total, here = beside(delta, (s, c), p + 1)
            w1[p, inner] = gamma[p] * here + dinv_c[p] * total
        for p in range(planes + 2):
            total, _ = beside(w1, (), p + 1)
            w2[p, inner] = gamma[p + 1] * delta[s, c, p + 2, inner] + dinv_c[p + 1] * total

    def first(c, _):
        pass_copy(new0.at[c], c).wait_recv()
        for p in range(planes):
            value = new0[c, p]
            out[0, c, p] = value
            delta[0, c, p + 3, inner] = value - states[0, c, p]
        start(lambda way: delta_copy(0, c, way))
        return 0

    lax.fori_loop(0, n_comp, first, 0)

    def second(c, _):
        arrived(lambda way: delta_copy(0, c, way))
        coarse_before(0, c)
        for p in range(planes):
            value = coarse(0, c, p) + v[end, 0, c, p + 1, inner]
            out[1, c, p] = value
            delta[1, c, p + 3, inner] = value - states[1, c, p]

        @pl.when(rank < n_tm - 1)
        def _():
            start(lambda way: delta_copy(1, c, way))

        return 0

    lax.fori_loop(0, n_comp, second, 0)

    @pl.when(rank < n_tm - 1)
    def _():
        def third(c, _):
            arrived(lambda way: delta_copy(1, c, way))
            coarse_before(1, c)
            for p in range(planes):
                passed[c, p] = coarse(1, c, p) + v[end, 1, c, p + 1, inner]
            pass_copy(passed.at[c], c).start()
            return 0

        lax.fori_loop(0, n_comp, third, 0)

    def leave(i, _):
        s, c = i // n_comp, i % n_comp
        sent(lambda way: halo_copy(1 - end, s, c, way))
        return 0

    lax.fori_loop(0, n_slice * n_comp, leave, 0)
    sent(cond_copy)
    all_of(*name_refs).wait_send()
    for gp in range(2):
        all_of(*gap_refs(gp)).wait_send()
    for c in range(n_comp):
        sent(lambda way: delta_copy(0, c, way))
        pass_copy(passed.at[c], c).wait_send()

        @pl.when(rank < n_tm - 1)
        def _():
            sent(lambda way: delta_copy(1, c, way))


def solution(mesh):
    n_space, n_tm = mesh.shape["space"], mesh.shape["tm"]

    def shards(states, sources, conductivity, gap_tile, gap_row):
        n_slice, n_comp, planes, rows, width = states.shape
        high = rows + 2 * PAD
        slots = n_space * CAP

        def f32(*shape):
            return pltpu.VMEM(shape, jnp.float32)

        def dma(*shape):
            return pltpu.SemaphoreType.DMA(shape)

        def body(*refs):
            kernel(n_space, n_tm, *refs)

        vmem = pl.BlockSpec(memory_space=pltpu.VMEM)
        return pl.pallas_call(
            body,
            out_shape=jax.ShapeDtypeStruct(states.shape, jnp.float32),
            in_specs=[vmem] * 5,
            out_specs=vmem,
            scratch_shapes=[
                f32(2, n_slice, n_comp, planes + 2, high, width),
                f32(n_slice, n_comp, planes, rows, width),
                f32(n_slice, n_comp, planes, rows, width),
                f32(planes, rows, width),
                f32(planes, rows, width),
                f32(planes + 4, high, width),
                f32(planes + 2, high, width),
                f32(n_slice, n_comp, planes + 6, high, width),
                f32(planes + 4, rows, width),
                f32(planes + 4, rows, width),
                f32(planes + 4, rows, width),
                f32(n_comp, planes, rows, width),
                f32(n_comp, planes, rows, width),
                f32(n_slice, slots, rows),
                f32(n_slice, rows, slots),
                f32(2, n_slice, slots, width),
                f32(2, n_slice, slots, width),
                f32(n_slice, slots, width),
                f32(n_slice, slots, width),
                f32(n_slice, rows, width),
                dma(2, n_slice, n_comp, 2), dma(2, n_slice, n_comp, 2),
                dma(2), dma(2), dma(1), dma(1), dma(2), dma(2),
                dma(n_slice, n_comp, 2), dma(n_slice, n_comp, 2), dma(n_comp), dma(n_comp),
            ],
            compiler_params=pltpu.CompilerParams(
                collective_id=0, has_side_effects=True, vmem_limit_bytes=48 * 1024 * 1024
            ),
        )(states, sources, conductivity, gap_tile, gap_row)

    return jax.shard_map(
        shards,
        mesh=mesh,
        in_specs=(
            P("tm", None, "space", None, None),
            P("tm", None, "space", None, None),
            P("space", None, None),
            P("tm", "space", None),
            P("tm", "space"),
        ),
        out_specs=P("tm", None, "space", None, None),
        check_vma=False,
    )
```

```python
import jax
import jax.numpy as jnp
from jax import lax
from jax.experimental import pallas as pl
from jax.experimental.pallas import tpu as pltpu
from jax.sharding import PartitionSpec as P

STEPS = 4
SWEEPS = 3
CAP = 8
PAD = 8

FREE = ((0, 6), (6, 9), (9, 12))
OPENING = (0, 1, 2, 3, 4, 5)
EARLY = 2
LAG = 2

INVERSE_STEP = 2.0
GAP_GAIN = 1.0
MESH = pl.DeviceIdType.MESH
HIGHEST = lax.Precision.HIGHEST


def kernel(
    n_space, n_tm,
    states, sources, conduct, gap_tile, gap_row,
    out,
    v, rhs, sig, alpha, dinv, w1, w2, delta, cond8, gamma, dinv_c, start_state, new0, passed,
    tile_in, row_in, pick, place, opening, opening_in, packed, landed, coupled,
    load_sem, halo_send, halo_recv, gap_send, gap_recv,
    cond_send, cond_recv, delta_send, delta_recv, pass_send, pass_recv, turn,
):
    me = lax.axis_index("space")
    rank = lax.axis_index("tm")
    n_slice, n_comp, planes, rows, width = states.shape
    slots = n_space * CAP
    inner = pl.ds(PAD, rows)
    left_dev = {"space": jnp.maximum(me - 1, 0)}
    right_dev = {"space": jnp.minimum(me + 1, n_space - 1)}
    has_left = me > 0
    has_right = me < n_space - 1
    lane = lax.broadcasted_iota(jnp.int32, (rows, width), 1)
    sub = lax.broadcasted_iota(jnp.int32, (rows, width), 0)

    n_field = n_slice * n_comp
    n_free = n_field - n_slice

    def place_of(s, c):
        return jnp.where(c == 0, n_free + s, s * (n_comp - 1) + c - 1)

    barrier = pltpu.get_barrier_semaphore()

    def greet(i, _):
        peer = lax.rem(me + i, n_space)
        pl.semaphore_signal(barrier, inc=1, device_id={"space": peer}, device_id_type=MESH)
        return 0

    lax.fori_loop(1, n_space, greet, 0)
    next_rank = lax.rem(rank + 1, n_tm)
    for peer in (next_rank, lax.rem(rank + n_tm - 1, n_tm)):
        pl.semaphore_signal(barrier, inc=1, device_id={"tm": peer}, device_id_type=MESH)

    fields = [(s, c) for s in range(n_slice) for c in range(n_comp)]
    slot_of = {(s, c): n_free + s if c == 0 else s * (n_comp - 1) + c - 1 for s, c in fields}
    tile_load = pltpu.make_async_copy(gap_tile, tile_in, load_sem.at[0])
    row_load = pltpu.make_async_copy(gap_row, row_in, load_sem.at[1])
    cond_load = pltpu.make_async_copy(conduct, cond8.at[pl.ds(2, planes)], load_sem.at[2])
    state_load = pltpu.make_async_copy(states, start_state, load_sem.at[3])
    field_loads = {
        (s, c): pltpu.make_async_copy(
            states.at[s, c], v.at[0, slot_of[s, c], pl.ds(1, planes), inner], load_sem.at[4 + slot_of[s, c]]
        )
        for s, c in fields
    }
    source_loads = {
        (s, c): pltpu.make_async_copy(
            sources.at[s, c], sig.at[slot_of[s, c]], load_sem.at[4 + n_field + slot_of[s, c]]
        )
        for s, c in fields
    }
    tile_load.start()
    row_load.start()
    cond_load.start()
    for at in sorted(fields, key=lambda at: at[1]):
        field_loads[at].start()
    for at in fields:
        source_loads[at].start()
    state_load.start()

    edge_rows = jnp.zeros((PAD, width), jnp.float32)
    no_plane = jnp.zeros((rows, width), jnp.float32)

    def pad_planes(ref, index, count):
        for p in range(count):
            ref[index + (p, pl.ds(0, PAD))] = edge_rows
            ref[index + (p, pl.ds(PAD + rows, PAD))] = edge_rows

    def pad_fields(i, _):
        s, c = i // n_comp, i % n_comp
        f = place_of(s, c)
        for par in range(2):
            pad_planes(v, (par, f), planes + 2)
        pad_planes(delta, (s, c), planes + 6)
        return 0

    lax.fori_loop(0, n_slice * n_comp, pad_fields, 0)
    pad_planes(w1, (), planes + 4)
    pad_planes(w2, (), planes + 2)

    def clear(first, past):
        def one(i, _):
            s, c = i // n_comp, i % n_comp
            for par in range(2):
                v[par, i, 0 if first else planes + 1, inner] = no_plane
            for p in range(3):
                delta[s, c, p if first else planes + 3 + p, inner] = no_plane
            return 0

        lax.fori_loop(0, n_slice * n_comp, one, 0)
        for p in range(2):
            cond8[p if first else planes + 2 + p] = no_plane

    @pl.when(jnp.logical_not(has_left))
    def _():
        clear(True, 0)

    @pl.when(jnp.logical_not(has_right))
    def _():
        clear(False, 0)

    tile_load.wait()
    row_load.wait()
    for s in range(n_slice):
        tile_row = jnp.broadcast_to(tile_in[s:s + 1].astype(jnp.float32), (rows, width))
        tile_col = tile_row.T
        before = jnp.where((tile_col == tile_row) & (sub < lane), 1.0, 0.0)
        position = jnp.sum(before, axis=0, keepdims=True)
        slot = tile_row[0:1] * CAP + position
        wide = lax.broadcasted_iota(jnp.int32, (slots, rows), 0).astype(jnp.float32)
        chosen = jnp.where(wide == slot, 1.0, 0.0)
        pick[s] = chosen
        target = row_in[s:s + 1].astype(jnp.float32) + 1.0
        named = jnp.sum(chosen * target, axis=1, keepdims=True)
        opening[n_slice + s] = jnp.broadcast_to(named, (slots, width))

    def packed_rows(s, par):
        return jnp.dot(
            pick[s], v[par, n_free + s, 1, inner], precision=HIGHEST, preferred_element_type=jnp.float32
        )

    for at in fields:
        field_loads[at].wait()
    for s in range(n_slice):
        opening[s] = packed_rows(s, 0)

    def fine_coefficients():
        for p in range(planes):
            rate = INVERSE_STEP * cond8[p + 2]
            inverse = 1.0 / (rate + 6.0)
            dinv[p] = inverse
            alpha[p] = rate * inverse
        for at in fields:
            source_loads[at].wait()

        def scaled(f, _):
            for p in range(planes):
                sig[f, p] = sig[f, p] * dinv[p]
            return 0

        lax.fori_loop(0, n_field, scaled, 0)

    cond_load.wait()
    pl.semaphore_wait(barrier, n_space - 1 + 2)

    def halo_copy(par, f, way):
        return pltpu.make_async_remote_copy(
            src_ref=v.at[par, f, 1 if way == 0 else planes, inner],
            dst_ref=v.at[par, f, planes + 1 if way == 0 else 0, inner],
            send_sem=halo_send.at[par, f, way],
            recv_sem=halo_recv.at[par, f, way],
            device_id=left_dev if way == 0 else right_dev,
            device_id_type=MESH,
        )

    def delta_copy(s, c, way):
        return pltpu.make_async_remote_copy(
            src_ref=delta.at[s, c, pl.ds(3 if way == 0 else planes, 3), inner],
            dst_ref=delta.at[s, c, pl.ds(planes + 3 if way == 0 else 0, 3), inner],
            send_sem=delta_send.at[s, c, way],
            recv_sem=delta_recv.at[s, c, way],
            device_id=left_dev if way == 0 else right_dev,
            device_id_type=MESH,
        )

    def cond_copy(way):
        return pltpu.make_async_remote_copy(
            src_ref=cond8.at[pl.ds(2 if way == 0 else planes, 2)],
            dst_ref=cond8.at[pl.ds(planes + 2 if way == 0 else 0, 2)],
            send_sem=cond_send.at[way],
            recv_sem=cond_recv.at[way],
            device_id=left_dev if way == 0 else right_dev,
            device_id_type=MESH,
        )

    def start(copy):
        @pl.when(has_left)
        def _():
            copy(0).start()

        @pl.when(has_right)
        def _():
            copy(1).start()

    def arrived(copy):
        @pl.when(has_right)
        def _():
            copy(0).wait_recv()

        @pl.when(has_left)
        def _():
            copy(1).wait_recv()

    def sent(copy):
        @pl.when(has_left)
        def _():
            copy(0).wait_send()

        @pl.when(has_right)
        def _():
            copy(1).wait_send()

    def scatter(source, landing, send_sem, recv_sem):
        def one(i, _):
            peer = lax.rem(me + i, n_space)
            pltpu.make_async_remote_copy(
                src_ref=source.at[:, pl.ds(pl.multiple_of(peer * CAP, CAP), CAP)],
                dst_ref=landing.at[:, pl.ds(pl.multiple_of(me * CAP, CAP), CAP)],
                send_sem=send_sem,
                recv_sem=recv_sem,
                device_id={"space": peer},
                device_id_type=MESH,
            ).start()
            return 0

        lax.fori_loop(1, n_space, one, 0)
        own = pl.ds(pl.multiple_of(me * CAP, CAP), CAP)
        for s in range(source.shape[0]):
            landing[s, own] = source[s, own]

    def all_of(source, landing, send_sem, recv_sem):
        most = pl.ds(0, (n_space - 1) * CAP)
        return pltpu.make_async_remote_copy(
            src_ref=source.at[:, most],
            dst_ref=landing.at[:, most],
            send_sem=send_sem,
            recv_sem=recv_sem,
            device_id=left_dev,
            device_id_type=MESH,
        )

    def gap_refs(gp):
        return packed.at[gp], landed.at[gp], gap_send.at[gp], gap_recv.at[gp]

    for f in OPENING:
        start(lambda way: halo_copy(0, f, way))
    opening_refs = (opening, opening_in, gap_send.at[2], gap_recv.at[2])
    scatter(*opening_refs)
    start(cond_copy)
    fine_coefficients()

    def beside(ref, index, p):
        here = ref[index + (p, inner)]
        total = ref[index + (p - 1, inner)] + ref[index + (p + 1, inner)]
        total = total + ref[index + (p, pl.ds(PAD - 1, rows))] + ref[index + (p, pl.ds(PAD + 1, rows))]
        total = total + jnp.where(lane == 0, 0.0, pltpu.roll(here, 1, 1))
        total = total + jnp.where(lane == width - 1, 0.0, pltpu.roll(here, width - 1, 1))
        return total, here

    def task(step, sweep, f, tied):
        count = step * SWEEPS + sweep
        par = lax.rem(count, 2)
        onto = 1 - par

        @pl.when(sweep == 0)
        def _():
            for p in range(planes):
                base = alpha[p] * v[par, f, p + 1, inner] + sig[f, p]
                if tied and p == 0:
                    base = base + dinv[0] * coupled[f - n_free]
                rhs[f, p] = base

        arrived(lambda way: halo_copy(par, f, way))

        @pl.when(count > 0)
        def _():
            sent(lambda way: halo_copy(onto, f, way))

        def plane(p):
            total, _ = beside(v, (par, f), p)
            v[onto, f, p, inner] = rhs[f, p - 1] + dinv[p - 1] * total

        plane(1)
        plane(planes)

        @pl.when((step < STEPS - 1) | (sweep < SWEEPS - 1))
        def _():
            start(lambda way: halo_copy(onto, f, way))

        for p in range(2, planes):
            plane(p)

    def coarse_coefficients():
        arrived(cond_copy)
        for p in range(planes + 4):
            rate = INVERSE_STEP * cond8[p] / STEPS
            inverse = 1.0 / (rate + 6.0)
            if p < 2:
                inverse = jnp.where(has_left, inverse, 0.0)
            if p >= planes + 2:
                inverse = jnp.where(has_right, inverse, 0.0)
            dinv_c[p] = inverse
            gamma[p] = rate * inverse

    state_load.wait()

    def pass_copy(source, c):
        return pltpu.make_async_remote_copy(
            src_ref=source,
            dst_ref=new0.at[c],
            send_sem=pass_send.at[c],
            recv_sem=pass_recv.at[c],
            device_id={"tm": next_rank},
            device_id_type=MESH,
        )

    def first(c, _):
        pass_copy(new0.at[c], c).wait_recv()
        for p in range(planes):
            value = new0[c, p]
            out[0, c, p] = value
            delta[0, c, p + 3, inner] = value - start_state[0, c, p]
        start(lambda way: delta_copy(0, c, way))
        return 0

    def couple(landing):
        for s in range(n_slice):
            coupled[s] = GAP_GAIN * jnp.dot(
                place[s], landing[s], precision=HIGHEST, preferred_element_type=jnp.float32
            )

    ahead = rank == n_tm - 1
    behind = rank == n_tm - 2
    beside_rank = lax.rem(rank + n_tm - 1, n_tm)

    def keep_pace(count):
        @pl.when(ahead & (count > 0) & (lax.rem(count, LAG) == 0))
        def _():
            pl.semaphore_signal(turn, inc=1, device_id={"tm": beside_rank}, device_id_type=MESH)

        @pl.when(behind & (count > 0) & (count <= STEPS * SWEEPS // LAG))
        def _():
            pl.semaphore_wait(turn, 1)

    def one_step(step, _):
        gp = lax.rem(step, 2)

        for sweep in range(SWEEPS):
            keep_pace(step * SWEEPS + sweep)

            def free(n, _):
                task(step, n // 4, n % 4, False)
                return 0

            lax.fori_loop(*FREE[sweep], free, 0)
            if sweep == 0:

                @pl.when(step == 0)
                def _():
                    all_of(*opening_refs).wait_recv()
                    for s in range(n_slice):
                        for part in range(slots // width):
                            held = opening_in[n_slice + s, pl.ds(part * width, width)]
                            hit = jnp.where(held == (lane + 1).astype(jnp.float32), 1.0, 0.0)
                            place[s, :, pl.ds(part * width, width)] = hit.T
                    couple(opening_in)

                @pl.when(step > 0)
                def _():
                    all_of(*gap_refs(gp)).wait_recv()
                    couple(landed.at[gp])

            if sweep == EARLY:
                @pl.when((rank == 0) & (step == STEPS - 1))
                def _():
                    lax.fori_loop(0, n_comp, first, 0)

            def tied(s, _, sweep=sweep):
                task(step, sweep, n_free + s, True)
                return 0

            lax.fori_loop(0, n_slice, tied, 0)

        @pl.when(step < STEPS - 1)
        def _():
            later = 1 - gp

            @pl.when(step > 1)
            def _():
                all_of(*gap_refs(later)).wait_send()

            for s in range(n_slice):
                packed[later, s] = packed_rows(s, lax.rem((step + 1) * SWEEPS, 2))
            scatter(*gap_refs(later))

        @pl.when(step == 0)
        def _():
            coarse_coefficients()

        return 0

    lax.fori_loop(0, STEPS, one_step, 0)
    keep_pace(jnp.int32(STEPS * SWEEPS))
    end = (STEPS * SWEEPS) % 2

    @pl.when(rank == n_tm - 1)
    def _():
        def one(c, _):
            pass_copy(v.at[end, place_of(n_slice - 1, c), pl.ds(1, planes), inner], c).start()
            return 0

        lax.fori_loop(0, n_comp, one, 0)

    def coarse(s, c, p):
        total, _ = beside(w2, (), p + 1)
        return gamma[p + 2] * delta[s, c, p + 3, inner] + dinv_c[p + 2] * total

    def coarse_before(s, c):
        for p in range(planes + 4):
            total, here = beside(delta, (s, c), p + 1)
            w1[p, inner] = gamma[p] * here + dinv_c[p] * total
        for p in range(planes + 2):
            total, _ = beside(w1, (), p + 1)
            w2[p, inner] = gamma[p + 1] * delta[s, c, p + 2, inner] + dinv_c[p + 1] * total

    @pl.when(rank > 0)
    def _():
        lax.fori_loop(0, n_comp, first, 0)

    def second(c, _):
        arrived(lambda way: delta_copy(0, c, way))
        coarse_before(0, c)
        for p in range(planes):
            value = coarse(0, c, p) + v[end, place_of(0, c), p + 1, inner]
            out[1, c, p] = value
            delta[1, c, p + 3, inner] = value - start_state[1, c, p]

        @pl.when(rank < n_tm - 1)
        def _():
            start(lambda way: delta_copy(1, c, way))

        return 0

    lax.fori_loop(0, n_comp, second, 0)

    @pl.when(rank < n_tm - 1)
    def _():
        def third(c, _):
            arrived(lambda way: delta_copy(1, c, way))
            coarse_before(1, c)
            for p in range(planes):
                passed[c, p] = coarse(1, c, p) + v[end, place_of(1, c), p + 1, inner]
            pass_copy(passed.at[c], c).start()
            return 0

        lax.fori_loop(0, n_comp, third, 0)

    for f in range(n_field):
        sent(lambda way: halo_copy(1 - end, f, way))
    sent(cond_copy)
    all_of(*opening_refs).wait_send()
    for gp in range(2):
        all_of(*gap_refs(gp)).wait_send()
    for c in range(n_comp):
        sent(lambda way: delta_copy(0, c, way))
        pass_copy(passed.at[c], c).wait_send()

        @pl.when(rank < n_tm - 1)
        def _():
            sent(lambda way: delta_copy(1, c, way))


def solution(mesh):
    n_space, n_tm = mesh.shape["space"], mesh.shape["tm"]

    def shards(states, sources, conductivity, gap_tile, gap_row):
        n_slice, n_comp, planes, rows, width = states.shape
        high = rows + 2 * PAD
        slots = n_space * CAP

        def f32(*shape):
            return pltpu.VMEM(shape, jnp.float32)

        def dma(*shape):
            return pltpu.SemaphoreType.DMA(shape)

        def body(*refs):
            kernel(n_space, n_tm, *refs)

        vmem = pl.BlockSpec(memory_space=pltpu.VMEM)
        return pl.pallas_call(
            body,
            out_shape=jax.ShapeDtypeStruct(states.shape, jnp.float32),
            in_specs=[pl.BlockSpec(memory_space=pl.ANY)] * 5,
            out_specs=vmem,
            scratch_shapes=[
                f32(2, n_slice * n_comp, planes + 2, high, width),
                f32(n_slice * n_comp, planes, rows, width),
                f32(n_slice * n_comp, planes, rows, width),
                f32(planes, rows, width),
                f32(planes, rows, width),
                f32(planes + 4, high, width),
                f32(planes + 2, high, width),
                f32(n_slice, n_comp, planes + 6, high, width),
                f32(planes + 4, rows, width),
                f32(planes + 4, rows, width),
                f32(planes + 4, rows, width),
                f32(n_slice, n_comp, planes, rows, width),
                f32(n_comp, planes, rows, width),
                f32(n_comp, planes, rows, width),
                pltpu.VMEM((n_slice, rows), jnp.int32),
                pltpu.VMEM((n_slice, rows), jnp.int32),
                f32(n_slice, slots, rows),
                f32(n_slice, rows, slots),
                f32(2 * n_slice, slots, width),
                f32(2 * n_slice, slots, width),
                f32(2, n_slice, slots, width),
                f32(2, n_slice, slots, width),
                f32(n_slice, rows, width),
                dma(4 + 2 * n_slice * n_comp), dma(2, n_slice * n_comp, 2), dma(2, n_slice * n_comp, 2),
                dma(3), dma(3), dma(2), dma(2),
                dma(n_slice, n_comp, 2), dma(n_slice, n_comp, 2), dma(n_comp), dma(n_comp),
                pltpu.SemaphoreType.REGULAR,
            ],
            compiler_params=pltpu.CompilerParams(
                collective_id=0, has_side_effects=True, vmem_limit_bytes=56 * 1024 * 1024
            ),
        )(states, sources, conductivity, gap_tile[:, :, 0], gap_row)

    return jax.shard_map(
        shards,
        mesh=mesh,
        in_specs=(
            P("tm", None, "space", None, None),
            P("tm", None, "space", None, None),
            P("space", None, None),
            P("tm", "space", None),
            P("tm", "space"),
        ),
        out_specs=P("tm", None, "space", None, None),
        check_vma=False,
    )
```

```python
import jax
import jax.numpy as jnp
from jax import lax
from jax.experimental import pallas as pl
from jax.experimental.pallas import tpu as pltpu
from jax.sharding import PartitionSpec as P

STEPS = 4
SWEEPS = 3
CAP = 8
PAD = 8

FREE = ((0, 6), (6, 9), (9, 12))
OPENING = (0, 1, 2, 3, 4, 5)
EARLY = 2
LEADS = (1, 4)

INVERSE_STEP = 2.0
GAP_GAIN = 1.0
MESH = pl.DeviceIdType.MESH
HIGHEST = lax.Precision.HIGHEST


def kernel(
    n_space, n_tm,
    states, sources, conduct, gap_tile, gap_row,
    out,
    v, rhs, sig, alpha, dinv, w1, w2, delta, cond8, gamma, dinv_c, start_state, new0, passed,
    tile_in, row_in, pick, place, opening, opening_in, packed, landed, coupled,
    load_sem, halo_send, halo_recv, gap_send, gap_recv,
    cond_send, cond_recv, delta_send, delta_recv, pass_send, pass_recv, turn,
):
    me = lax.axis_index("space")
    rank = lax.axis_index("tm")
    n_slice, n_comp, planes, rows, width = states.shape
    slots = n_space * CAP
    inner = pl.ds(PAD, rows)
    left_dev = {"space": jnp.maximum(me - 1, 0)}
    right_dev = {"space": jnp.minimum(me + 1, n_space - 1)}
    has_left = me > 0
    has_right = me < n_space - 1
    lane = lax.broadcasted_iota(jnp.int32, (rows, width), 1)
    sub = lax.broadcasted_iota(jnp.int32, (rows, width), 0)

    n_field = n_slice * n_comp
    n_free = n_field - n_slice

    def place_of(s, c):
        return jnp.where(c == 0, n_free + s, s * (n_comp - 1) + c - 1)

    barrier = pltpu.get_barrier_semaphore()

    def greet(i, _):
        peer = lax.rem(me + i, n_space)
        pl.semaphore_signal(barrier, inc=1, device_id={"space": peer}, device_id_type=MESH)
        return 0

    lax.fori_loop(1, n_space, greet, 0)
    next_rank = lax.rem(rank + 1, n_tm)
    for peer in (next_rank, lax.rem(rank + n_tm - 1, n_tm)):
        pl.semaphore_signal(barrier, inc=1, device_id={"tm": peer}, device_id_type=MESH)

    fields = [(s, c) for s in range(n_slice) for c in range(n_comp)]
    slot_of = {(s, c): n_free + s if c == 0 else s * (n_comp - 1) + c - 1 for s, c in fields}
    tile_load = pltpu.make_async_copy(gap_tile, tile_in, load_sem.at[0])
    row_load = pltpu.make_async_copy(gap_row, row_in, load_sem.at[1])
    cond_load = pltpu.make_async_copy(conduct, cond8.at[pl.ds(2, planes)], load_sem.at[2])
    state_load = pltpu.make_async_copy(states, start_state, load_sem.at[3])
    field_loads = {
        (s, c): pltpu.make_async_copy(
            states.at[s, c], v.at[0, slot_of[s, c], pl.ds(1, planes), inner], load_sem.at[4 + slot_of[s, c]]
        )
        for s, c in fields
    }
    source_loads = {
        (s, c): pltpu.make_async_copy(
            sources.at[s, c], sig.at[slot_of[s, c]], load_sem.at[4 + n_field + slot_of[s, c]]
        )
        for s, c in fields
    }
    tile_load.start()
    row_load.start()
    cond_load.start()
    for at in sorted(fields, key=lambda at: at[1]):
        field_loads[at].start()
    for at in fields:
        source_loads[at].start()
    state_load.start()

    edge_rows = jnp.zeros((PAD, width), jnp.float32)
    no_plane = jnp.zeros((rows, width), jnp.float32)

    def pad_planes(ref, index, count):
        for p in range(count):
            ref[index + (p, pl.ds(0, PAD))] = edge_rows
            ref[index + (p, pl.ds(PAD + rows, PAD))] = edge_rows

    def pad_fields(i, _):
        s, c = i // n_comp, i % n_comp
        f = place_of(s, c)
        for par in range(2):
            pad_planes(v, (par, f), planes + 2)
        pad_planes(delta, (s, c), planes + 6)
        return 0

    lax.fori_loop(0, n_slice * n_comp, pad_fields, 0)
    pad_planes(w1, (), planes + 4)
    pad_planes(w2, (), planes + 2)

    def clear(first, past):
        def one(i, _):
            s, c = i // n_comp, i % n_comp
            for par in range(2):
                v[par, i, 0 if first else planes + 1, inner] = no_plane
            for p in range(3):
                delta[s, c, p if first else planes + 3 + p, inner] = no_plane
            return 0

        lax.fori_loop(0, n_slice * n_comp, one, 0)
        for p in range(2):
            cond8[p if first else planes + 2 + p] = no_plane

    @pl.when(jnp.logical_not(has_left))
    def _():
        clear(True, 0)

    @pl.when(jnp.logical_not(has_right))
    def _():
        clear(False, 0)

    tile_load.wait()
    row_load.wait()
    names = []
    for s in range(n_slice):
        tile_row = jnp.broadcast_to(tile_in[s:s + 1].astype(jnp.float32), (rows, width))
        tile_col = tile_row.T
        before = jnp.where((tile_col == tile_row) & (sub < lane), 1.0, 0.0)
        position = jnp.sum(before, axis=0, keepdims=True)
        slot = tile_row[0:1] * CAP + position
        wide = lax.broadcasted_iota(jnp.int32, (slots, rows), 0).astype(jnp.float32)
        chosen = jnp.where(wide == slot, 1.0, 0.0)
        pick[s] = chosen
        target = row_in[s:s + 1].astype(jnp.float32) + 1.0
        named = jnp.sum(chosen * target, axis=1, keepdims=True)
        names.append(jnp.broadcast_to(named, (slots, width)))
    half = width // n_slice
    opening[n_slice] = jnp.where(lax.broadcasted_iota(jnp.int32, (slots, width), 1) < half, *names)

    def packed_rows(s, par):
        return jnp.dot(
            pick[s], v[par, n_free + s, 1, inner], precision=HIGHEST, preferred_element_type=jnp.float32
        )

    for at in fields:
        field_loads[at].wait()
    for s in range(n_slice):
        opening[s] = packed_rows(s, 0)

    def fine_coefficients():
        for p in range(planes):
            rate = INVERSE_STEP * cond8[p + 2]
            inverse = 1.0 / (rate + 6.0)
            dinv[p] = inverse
            alpha[p] = rate * inverse
        for at in fields:
            source_loads[at].wait()

        def scaled(f, _):
            for p in range(planes):
                sig[f, p] = sig[f, p] * dinv[p]
            return 0

        lax.fori_loop(0, n_field, scaled, 0)

    cond_load.wait()
    pl.semaphore_wait(barrier, n_space - 1 + 2)

    def halo_copy(par, f, way):
        return pltpu.make_async_remote_copy(
            src_ref=v.at[par, f, 1 if way == 0 else planes, inner],
            dst_ref=v.at[par, f, planes + 1 if way == 0 else 0, inner],
            send_sem=halo_send.at[par, f, way],
            recv_sem=halo_recv.at[par, f, way],
            device_id=left_dev if way == 0 else right_dev,
            device_id_type=MESH,
        )

    def delta_copy(s, c, way):
        return pltpu.make_async_remote_copy(
            src_ref=delta.at[s, c, pl.ds(3 if way == 0 else planes, 3), inner],
            dst_ref=delta.at[s, c, pl.ds(planes + 3 if way == 0 else 0, 3), inner],
            send_sem=delta_send.at[s, c, way],
            recv_sem=delta_recv.at[s, c, way],
            device_id=left_dev if way == 0 else right_dev,
            device_id_type=MESH,
        )

    def cond_copy(way):
        return pltpu.make_async_remote_copy(
            src_ref=cond8.at[pl.ds(2 if way == 0 else planes, 2)],
            dst_ref=cond8.at[pl.ds(planes + 2 if way == 0 else 0, 2)],
            send_sem=cond_send.at[way],
            recv_sem=cond_recv.at[way],
            device_id=left_dev if way == 0 else right_dev,
            device_id_type=MESH,
        )

    def start(copy):
        @pl.when(has_left)
        def _():
            copy(0).start()

        @pl.when(has_right)
        def _():
            copy(1).start()

    def arrived(copy):
        @pl.when(has_right)
        def _():
            copy(0).wait_recv()

        @pl.when(has_left)
        def _():
            copy(1).wait_recv()

    def sent(copy):
        @pl.when(has_left)
        def _():
            copy(0).wait_send()

        @pl.when(has_right)
        def _():
            copy(1).wait_send()

    def scatter(source, landing, send_sem, recv_sem):
        def one(i, _):
            peer = lax.rem(me + i, n_space)
            pltpu.make_async_remote_copy(
                src_ref=source.at[:, pl.ds(pl.multiple_of(peer * CAP, CAP), CAP)],
                dst_ref=landing.at[:, pl.ds(pl.multiple_of(me * CAP, CAP), CAP)],
                send_sem=send_sem,
                recv_sem=recv_sem,
                device_id={"space": peer},
                device_id_type=MESH,
            ).start()
            return 0

        lax.fori_loop(1, n_space, one, 0)
        own = pl.ds(pl.multiple_of(me * CAP, CAP), CAP)
        for s in range(source.shape[0]):
            landing[s, own] = source[s, own]

    def all_of(source, landing, send_sem, recv_sem):
        most = pl.ds(0, (n_space - 1) * CAP)
        return pltpu.make_async_remote_copy(
            src_ref=source.at[:, most],
            dst_ref=landing.at[:, most],
            send_sem=send_sem,
            recv_sem=recv_sem,
            device_id=left_dev,
            device_id_type=MESH,
        )

    def gap_refs(gp):
        return packed.at[gp], landed.at[gp], gap_send.at[gp], gap_recv.at[gp]

    for f in OPENING:
        start(lambda way: halo_copy(0, f, way))
    opening_refs = (opening, opening_in, gap_send.at[2], gap_recv.at[2])
    scatter(*opening_refs)
    start(cond_copy)
    fine_coefficients()

    def beside(ref, index, p):
        here = ref[index + (p, inner)]
        total = ref[index + (p - 1, inner)] + ref[index + (p + 1, inner)]
        total = total + ref[index + (p, pl.ds(PAD - 1, rows))] + ref[index + (p, pl.ds(PAD + 1, rows))]
        total = total + jnp.where(lane == 0, 0.0, pltpu.roll(here, 1, 1))
        total = total + jnp.where(lane == width - 1, 0.0, pltpu.roll(here, width - 1, 1))
        return total, here

    def task(step, sweep, f, tied):
        count = step * SWEEPS + sweep
        par = lax.rem(count, 2)
        onto = 1 - par

        @pl.when(sweep == 0)
        def _():
            for p in range(planes):
                base = alpha[p] * v[par, f, p + 1, inner] + sig[f, p]
                if tied and p == 0:
                    base = base + dinv[0] * coupled[f - n_free]
                rhs[f, p] = base

        arrived(lambda way: halo_copy(par, f, way))

        @pl.when(count > 0)
        def _():
            sent(lambda way: halo_copy(onto, f, way))

        def plane(p):
            total, _ = beside(v, (par, f), p)
            v[onto, f, p, inner] = rhs[f, p - 1] + dinv[p - 1] * total

        plane(1)
        plane(planes)

        @pl.when((step < STEPS - 1) | (sweep < SWEEPS - 1))
        def _():
            start(lambda way: halo_copy(onto, f, way))

        for p in range(2, planes):
            plane(p)

    def coarse_coefficients():
        arrived(cond_copy)
        for p in range(planes + 4):
            rate = INVERSE_STEP * cond8[p] / STEPS
            inverse = 1.0 / (rate + 6.0)
            if p < 2:
                inverse = jnp.where(has_left, inverse, 0.0)
            if p >= planes + 2:
                inverse = jnp.where(has_right, inverse, 0.0)
            dinv_c[p] = inverse
            gamma[p] = rate * inverse

    state_load.wait()

    def pass_copy(source, c):
        return pltpu.make_async_remote_copy(
            src_ref=source,
            dst_ref=new0.at[c],
            send_sem=pass_send.at[c],
            recv_sem=pass_recv.at[c],
            device_id={"tm": next_rank},
            device_id_type=MESH,
        )

    def first(c, _):
        pass_copy(new0.at[c], c).wait_recv()
        for p in range(planes):
            value = new0[c, p]
            out[0, c, p] = value
            delta[0, c, p + 3, inner] = value - start_state[0, c, p]
        start(lambda way: delta_copy(0, c, way))
        return 0

    def couple(landing):
        for s in range(n_slice):
            coupled[s] = GAP_GAIN * jnp.dot(
                place[s], landing[s], precision=HIGHEST, preferred_element_type=jnp.float32
            )

    leads = ((0, 1, LEADS[0]), (n_tm - 1, n_tm - 2, LEADS[1]))

    def keep_pace(count):
        for leader, follower, lead in leads:

            @pl.when((rank == leader) & (count >= lead) & (count < STEPS * SWEEPS))
            def _():
                pl.semaphore_signal(turn, inc=1, device_id={"tm": follower}, device_id_type=MESH)

            @pl.when((rank == follower) & (count + lead < STEPS * SWEEPS))
            def _():
                pl.semaphore_wait(turn, 1)

    def one_step(step, _):
        gp = lax.rem(step, 2)

        for sweep in range(SWEEPS):
            keep_pace(step * SWEEPS + sweep)

            def free(n, _):
                task(step, n // 4, n % 4, False)
                return 0

            lax.fori_loop(*FREE[sweep], free, 0)
            if sweep == 0:

                @pl.when(step == 0)
                def _():
                    all_of(*opening_refs).wait_recv()
                    for s in range(n_slice):
                        for part in range(slots // width):
                            held = opening_in[n_slice, pl.ds(part * width, width)]
                            held = jnp.broadcast_to(held[:, s * half:s * half + 1], (width, width))
                            hit = jnp.where(held == (lane + 1).astype(jnp.float32), 1.0, 0.0)
                            place[s, :, pl.ds(part * width, width)] = hit.T
                    couple(opening_in)

                @pl.when(step > 0)
                def _():
                    all_of(*gap_refs(gp)).wait_recv()
                    couple(landed.at[gp])

            if sweep == EARLY:
                @pl.when((rank == 0) & (step == STEPS - 1))
                def _():
                    lax.fori_loop(0, n_comp, first, 0)

            def tied(s, _, sweep=sweep):
                task(step, sweep, n_free + s, True)
                return 0

            lax.fori_loop(0, n_slice, tied, 0)

        @pl.when(step < STEPS - 1)
        def _():
            later = 1 - gp

            @pl.when(step > 1)
            def _():
                all_of(*gap_refs(later)).wait_send()

            for s in range(n_slice):
                packed[later, s] = packed_rows(s, lax.rem((step + 1) * SWEEPS, 2))
            scatter(*gap_refs(later))

        @pl.when(step == 0)
        def _():
            coarse_coefficients()

        return 0

    lax.fori_loop(0, STEPS, one_step, 0)
    end = (STEPS * SWEEPS) % 2

    @pl.when(rank == n_tm - 1)
    def _():
        def one(c, _):
            pass_copy(v.at[end, place_of(n_slice - 1, c), pl.ds(1, planes), inner], c).start()
            return 0

        lax.fori_loop(0, n_comp, one, 0)

    def coarse(s, c, p):
        total, _ = beside(w2, (), p + 1)
        return gamma[p + 2] * delta[s, c, p + 3, inner] + dinv_c[p + 2] * total

    def coarse_before(s, c):
        for p in range(planes + 4):
            total, here = beside(delta, (s, c), p + 1)
            w1[p, inner] = gamma[p] * here + dinv_c[p] * total
        for p in range(planes + 2):
            total, _ = beside(w1, (), p + 1)
            w2[p, inner] = gamma[p + 1] * delta[s, c, p + 2, inner] + dinv_c[p + 1] * total

    @pl.when(rank > 0)
    def _():
        lax.fori_loop(0, n_comp, first, 0)

    def second(c, _):
        arrived(lambda way: delta_copy(0, c, way))
        coarse_before(0, c)
        for p in range(planes):
            value = coarse(0, c, p) + v[end, place_of(0, c), p + 1, inner]
            out[1, c, p] = value
            delta[1, c, p + 3, inner] = value - start_state[1, c, p]

        @pl.when(rank < n_tm - 1)
        def _():
            start(lambda way: delta_copy(1, c, way))

        return 0

    lax.fori_loop(0, n_comp, second, 0)

    @pl.when(rank < n_tm - 1)
    def _():
        def third(c, _):
            arrived(lambda way: delta_copy(1, c, way))
            coarse_before(1, c)
            for p in range(planes):
                passed[c, p] = coarse(1, c, p) + v[end, place_of(1, c), p + 1, inner]
            pass_copy(passed.at[c], c).start()
            return 0

        lax.fori_loop(0, n_comp, third, 0)

    for f in range(n_field):
        sent(lambda way: halo_copy(1 - end, f, way))
    sent(cond_copy)
    all_of(*opening_refs).wait_send()
    for gp in range(2):
        all_of(*gap_refs(gp)).wait_send()
    for c in range(n_comp):
        sent(lambda way: delta_copy(0, c, way))
        pass_copy(passed.at[c], c).wait_send()

        @pl.when(rank < n_tm - 1)
        def _():
            sent(lambda way: delta_copy(1, c, way))


def solution(mesh):
    n_space, n_tm = mesh.shape["space"], mesh.shape["tm"]

    def shards(states, sources, conductivity, gap_tile, gap_row):
        n_slice, n_comp, planes, rows, width = states.shape
        high = rows + 2 * PAD
        slots = n_space * CAP

        def f32(*shape):
            return pltpu.VMEM(shape, jnp.float32)

        def dma(*shape):
            return pltpu.SemaphoreType.DMA(shape)

        def body(*refs):
            kernel(n_space, n_tm, *refs)

        vmem = pl.BlockSpec(memory_space=pltpu.VMEM)
        return pl.pallas_call(
            body,
            out_shape=jax.ShapeDtypeStruct(states.shape, jnp.float32),
            in_specs=[pl.BlockSpec(memory_space=pl.ANY)] * 5,
            out_specs=vmem,
            scratch_shapes=[
                f32(2, n_slice * n_comp, planes + 2, high, width),
                f32(n_slice * n_comp, planes, rows, width),
                f32(n_slice * n_comp, planes, rows, width),
                f32(planes, rows, width),
                f32(planes, rows, width),
                f32(planes + 4, high, width),
                f32(planes + 2, high, width),
                f32(n_slice, n_comp, planes + 6, high, width),
                f32(planes + 4, rows, width),
                f32(planes + 4, rows, width),
                f32(planes + 4, rows, width),
                f32(n_slice, n_comp, planes, rows, width),
                f32(n_comp, planes, rows, width),
                f32(n_comp, planes, rows, width),
                pltpu.VMEM((n_slice, rows), jnp.int32),
                pltpu.VMEM((n_slice, rows), jnp.int32),
                f32(n_slice, slots, rows),
                f32(n_slice, rows, slots),
                f32(n_slice + 1, slots, width),
                f32(n_slice + 1, slots, width),
                f32(2, n_slice, slots, width),
                f32(2, n_slice, slots, width),
                f32(n_slice, rows, width),
                dma(4 + 2 * n_slice * n_comp), dma(2, n_slice * n_comp, 2), dma(2, n_slice * n_comp, 2),
                dma(3), dma(3), dma(2), dma(2),
                dma(n_slice, n_comp, 2), dma(n_slice, n_comp, 2), dma(n_comp), dma(n_comp),
                pltpu.SemaphoreType.REGULAR,
            ],
            compiler_params=pltpu.CompilerParams(
                collective_id=0, has_side_effects=True, vmem_limit_bytes=56 * 1024 * 1024
            ),
        )(states, sources, conductivity, gap_tile[:, :, 0], gap_row)

    return jax.shard_map(
        shards,
        mesh=mesh,
        in_specs=(
            P("tm", None, "space", None, None),
            P("tm", None, "space", None, None),
            P("space", None, None),
            P("tm", "space", None),
            P("tm", "space"),
        ),
        out_specs=P("tm", None, "space", None, None),
        check_vma=False,
    )
```

```python
import jax
import jax.numpy as jnp
from jax import lax
from jax.experimental import pallas as pl
from jax.experimental.pallas import tpu as pltpu
from jax.sharding import PartitionSpec as P

STEPS = 4
SWEEPS = 3
CAP = 8
PAD = 8

FREE = ((0, 6), (6, 9), (9, 12))
OPENING = (0, 1, 2, 3, 4, 5)
EARLY = 2
LEADS = (1, 4)

INVERSE_STEP = 2.0
GAP_GAIN = 1.0
MESH = pl.DeviceIdType.MESH
HIGHEST = lax.Precision.HIGHEST


def kernel(
    n_space, n_tm,
    states, sources, conduct, gap_tile, gap_row,
    out,
    v, rhs, sig, alpha, dinv, w1, w2, delta, cond8, gamma, dinv_c, start_state, new0, passed,
    tile_in, row_in, pick, place, opening, opening_in, packed, landed, coupled,
    load_sem, halo_send, halo_recv, gap_send, gap_recv,
    cond_send, cond_recv, delta_send, delta_recv, pass_send, pass_recv, turn,
):
    me = lax.axis_index("space")
    rank = lax.axis_index("tm")
    n_slice, n_comp, planes, rows, width = states.shape
    slots = n_space * CAP
    inner = pl.ds(PAD, rows)
    left_dev = {"space": jnp.maximum(me - 1, 0)}
    right_dev = {"space": jnp.minimum(me + 1, n_space - 1)}
    has_left = me > 0
    has_right = me < n_space - 1
    lane = lax.broadcasted_iota(jnp.int32, (rows, width), 1)
    sub = lax.broadcasted_iota(jnp.int32, (rows, width), 0)

    n_field = n_slice * n_comp
    n_free = n_field - n_slice

    def place_of(s, c):
        return jnp.where(c == 0, n_free + s, s * (n_comp - 1) + c - 1)

    barrier = pltpu.get_barrier_semaphore()

    def greet(i, _):
        peer = lax.rem(me + i, n_space)
        pl.semaphore_signal(barrier, inc=1, device_id={"space": peer}, device_id_type=MESH)
        return 0

    lax.fori_loop(1, n_space, greet, 0)
    next_rank = lax.rem(rank + 1, n_tm)
    for peer in (next_rank, lax.rem(rank + n_tm - 1, n_tm)):
        pl.semaphore_signal(barrier, inc=1, device_id={"tm": peer}, device_id_type=MESH)

    fields = [(s, c) for s in range(n_slice) for c in range(n_comp)]
    slot_of = {(s, c): n_free + s if c == 0 else s * (n_comp - 1) + c - 1 for s, c in fields}
    tile_load = pltpu.make_async_copy(gap_tile, tile_in, load_sem.at[0])
    row_load = pltpu.make_async_copy(gap_row, row_in, load_sem.at[1])
    cond_load = pltpu.make_async_copy(conduct, cond8.at[pl.ds(2, planes)], load_sem.at[2])
    state_load = pltpu.make_async_copy(states, start_state, load_sem.at[3])
    field_loads = {
        (s, c): pltpu.make_async_copy(
            states.at[s, c], v.at[0, slot_of[s, c], pl.ds(1, planes), inner], load_sem.at[4 + slot_of[s, c]]
        )
        for s, c in fields
    }
    source_loads = {
        (s, c): pltpu.make_async_copy(
            sources.at[s, c], sig.at[slot_of[s, c]], load_sem.at[4 + n_field + slot_of[s, c]]
        )
        for s, c in fields
    }
    tile_load.start()
    row_load.start()
    cond_load.start()
    for at in sorted(fields, key=lambda at: at[1]):
        field_loads[at].start()
    for at in fields:
        source_loads[at].start()
    state_load.start()

    edge_rows = jnp.zeros((PAD, width), jnp.float32)
    no_plane = jnp.zeros((rows, width), jnp.float32)

    def pad_planes(ref, index, count):
        for p in range(count):
            ref[index + (p, pl.ds(0, PAD))] = edge_rows
            ref[index + (p, pl.ds(PAD + rows, PAD))] = edge_rows

    def pad_fields(i, _):
        s, c = i // n_comp, i % n_comp
        f = place_of(s, c)
        for par in range(2):
            pad_planes(v, (par, f), planes + 2)
        pad_planes(delta, (s, c), planes + 6)
        return 0

    lax.fori_loop(0, n_slice * n_comp, pad_fields, 0)
    pad_planes(w1, (), planes + 4)
    pad_planes(w2, (), planes + 2)

    def clear(first, past):
        def one(i, _):
            s, c = i // n_comp, i % n_comp
            for par in range(2):
                v[par, i, 0 if first else planes + 1, inner] = no_plane
            for p in range(3):
                delta[s, c, p if first else planes + 3 + p, inner] = no_plane
            return 0

        lax.fori_loop(0, n_slice * n_comp, one, 0)
        for p in range(2):
            cond8[p if first else planes + 2 + p] = no_plane

    @pl.when(jnp.logical_not(has_left))
    def _():
        clear(True, 0)

    @pl.when(jnp.logical_not(has_right))
    def _():
        clear(False, 0)

    tile_load.wait()
    row_load.wait()
    names = []
    for s in range(n_slice):
        tile_row = jnp.broadcast_to(tile_in[s:s + 1].astype(jnp.float32), (rows, width))
        tile_col = tile_row.T
        before = jnp.where((tile_col == tile_row) & (sub < lane), 1.0, 0.0)
        position = jnp.sum(before, axis=0, keepdims=True)
        slot = tile_row[0:1] * CAP + position
        wide = lax.broadcasted_iota(jnp.int32, (slots, rows), 0).astype(jnp.float32)
        chosen = jnp.where(wide == slot, 1.0, 0.0)
        pick[s] = chosen
        target = row_in[s:s + 1].astype(jnp.float32) + 1.0
        named = jnp.sum(chosen * target, axis=1, keepdims=True)
        names.append(jnp.broadcast_to(named, (slots, width)))
    half = width // n_slice
    opening[n_slice] = jnp.where(lax.broadcasted_iota(jnp.int32, (slots, width), 1) < half, *names)

    def packed_rows(s, par):
        return jnp.dot(
            pick[s], v[par, n_free + s, 1, inner], precision=HIGHEST, preferred_element_type=jnp.float32
        )

    for at in fields:
        field_loads[at].wait()
    for s in range(n_slice):
        opening[s] = packed_rows(s, 0)

    def fine_coefficients():
        for p in range(planes):
            rate = INVERSE_STEP * cond8[p + 2]
            inverse = 1.0 / (rate + 6.0)
            dinv[p] = inverse
            alpha[p] = rate * inverse
        for at in fields:
            source_loads[at].wait()

        def scaled(f, _):
            for p in range(planes):
                sig[f, p] = sig[f, p] * dinv[p]
            return 0

        lax.fori_loop(0, n_field, scaled, 0)

    cond_load.wait()
    pl.semaphore_wait(barrier, n_space - 1 + 2)

    def halo_copy(par, f, way):
        return pltpu.make_async_remote_copy(
            src_ref=v.at[par, f, 1 if way == 0 else planes, inner],
            dst_ref=v.at[par, f, planes + 1 if way == 0 else 0, inner],
            send_sem=halo_send.at[par, f, way],
            recv_sem=halo_recv.at[par, f, way],
            device_id=left_dev if way == 0 else right_dev,
            device_id_type=MESH,
        )

    def delta_copy(s, c, way):
        return pltpu.make_async_remote_copy(
            src_ref=delta.at[s, c, pl.ds(3 if way == 0 else planes, 3), inner],
            dst_ref=delta.at[s, c, pl.ds(planes + 3 if way == 0 else 0, 3), inner],
            send_sem=delta_send.at[s, c, way],
            recv_sem=delta_recv.at[s, c, way],
            device_id=left_dev if way == 0 else right_dev,
            device_id_type=MESH,
        )

    def cond_copy(way):
        return pltpu.make_async_remote_copy(
            src_ref=cond8.at[pl.ds(2 if way == 0 else planes, 2)],
            dst_ref=cond8.at[pl.ds(planes + 2 if way == 0 else 0, 2)],
            send_sem=cond_send.at[way],
            recv_sem=cond_recv.at[way],
            device_id=left_dev if way == 0 else right_dev,
            device_id_type=MESH,
        )

    def start(copy):
        @pl.when(has_left)
        def _():
            copy(0).start()

        @pl.when(has_right)
        def _():
            copy(1).start()

    def arrived(copy):
        @pl.when(has_right)
        def _():
            copy(0).wait_recv()

        @pl.when(has_left)
        def _():
            copy(1).wait_recv()

    def sent(copy):
        @pl.when(has_left)
        def _():
            copy(0).wait_send()

        @pl.when(has_right)
        def _():
            copy(1).wait_send()

    def scatter(source, landing, send_sem, recv_sem):
        def one(i, _):
            peer = lax.rem(me + i, n_space)
            pltpu.make_async_remote_copy(
                src_ref=source.at[:, pl.ds(pl.multiple_of(peer * CAP, CAP), CAP)],
                dst_ref=landing.at[:, pl.ds(pl.multiple_of(me * CAP, CAP), CAP)],
                send_sem=send_sem,
                recv_sem=recv_sem,
                device_id={"space": peer},
                device_id_type=MESH,
            ).start()
            return 0

        lax.fori_loop(1, n_space, one, 0)
        own = pl.ds(pl.multiple_of(me * CAP, CAP), CAP)
        for s in range(source.shape[0]):
            landing[s, own] = source[s, own]

    def all_of(source, landing, send_sem, recv_sem):
        most = pl.ds(0, (n_space - 1) * CAP)
        return pltpu.make_async_remote_copy(
            src_ref=source.at[:, most],
            dst_ref=landing.at[:, most],
            send_sem=send_sem,
            recv_sem=recv_sem,
            device_id=left_dev,
            device_id_type=MESH,
        )

    def gap_refs(gp):
        return packed.at[gp], landed.at[gp], gap_send.at[gp], gap_recv.at[gp]

    for f in OPENING:
        start(lambda way: halo_copy(0, f, way))
    opening_refs = (opening, opening_in, gap_send.at[2], gap_recv.at[2])
    scatter(*opening_refs)
    start(cond_copy)
    fine_coefficients()

    def beside(ref, index, p):
        here = ref[index + (p, inner)]
        total = ref[index + (p - 1, inner)] + ref[index + (p + 1, inner)]
        total = total + ref[index + (p, pl.ds(PAD - 1, rows))] + ref[index + (p, pl.ds(PAD + 1, rows))]
        total = total + jnp.where(lane == 0, 0.0, pltpu.roll(here, 1, 1))
        total = total + jnp.where(lane == width - 1, 0.0, pltpu.roll(here, width - 1, 1))
        return total, here

    def task(step, sweep, f, tied):
        count = step * SWEEPS + sweep
        par = lax.rem(count, 2)
        onto = 1 - par

        @pl.when(sweep == 0)
        def _():
            for p in range(planes):
                base = alpha[p] * v[par, f, p + 1, inner] + sig[f, p]
                if tied and p == 0:
                    base = base + dinv[0] * coupled[f - n_free]
                rhs[f, p] = base

        arrived(lambda way: halo_copy(par, f, way))

        @pl.when(count > 0)
        def _():
            sent(lambda way: halo_copy(onto, f, way))

        def plane(p):
            total, _ = beside(v, (par, f), p)
            v[onto, f, p, inner] = rhs[f, p - 1] + dinv[p - 1] * total

        plane(1)
        plane(planes)

        @pl.when((step < STEPS - 1) | (sweep < SWEEPS - 1))
        def _():
            start(lambda way: halo_copy(onto, f, way))

        for p in range(2, planes):
            plane(p)

    def coarse_coefficients():
        arrived(cond_copy)
        for p in range(planes + 4):
            rate = INVERSE_STEP * cond8[p] / STEPS
            inverse = 1.0 / (rate + 6.0)
            if p < 2:
                inverse = jnp.where(has_left, inverse, 0.0)
            if p >= planes + 2:
                inverse = jnp.where(has_right, inverse, 0.0)
            dinv_c[p] = inverse
            gamma[p] = rate * inverse

    state_load.wait()
    end = (STEPS * SWEEPS) % 2

    def pass_copy(source, c):
        return pltpu.make_async_remote_copy(
            src_ref=source,
            dst_ref=new0.at[c],
            send_sem=pass_send.at[c],
            recv_sem=pass_recv.at[c],
            device_id={"tm": next_rank},
            device_id_type=MESH,
        )

    def first(c, _):
        pass_copy(new0.at[c], c).wait_recv()
        for p in range(planes):
            value = new0[c, p]
            out[0, c, p] = value
            delta[0, c, p + 3, inner] = value - start_state[0, c, p]
        start(lambda way: delta_copy(0, c, way))
        return 0

    def coarse(s, c, p):
        total, _ = beside(w2, (), p + 1)
        return gamma[p + 2] * delta[s, c, p + 3, inner] + dinv_c[p + 2] * total

    def coarse_before(s, c):
        for p in range(planes + 4):
            total, here = beside(delta, (s, c), p + 1)
            w1[p, inner] = gamma[p] * here + dinv_c[p] * total
        for p in range(planes + 2):
            total, _ = beside(w1, (), p + 1)
            w2[p, inner] = gamma[p + 1] * delta[s, c, p + 2, inner] + dinv_c[p + 1] * total

    def second(c, _):
        arrived(lambda way: delta_copy(0, c, way))
        coarse_before(0, c)
        for p in range(planes):
            value = coarse(0, c, p) + v[end, place_of(0, c), p + 1, inner]
            out[1, c, p] = value
            delta[1, c, p + 3, inner] = value - start_state[1, c, p]

        @pl.when(rank < n_tm - 1)
        def _():
            start(lambda way: delta_copy(1, c, way))

        return 0

    def by_component(first_at, past, act):
        def one(i, _):
            return act(lax.rem(i + 1, n_comp), 0)

        lax.fori_loop(first_at, past, one, 0)

    def couple(landing):
        for s in range(n_slice):
            coupled[s] = GAP_GAIN * jnp.dot(
                place[s], landing[s], precision=HIGHEST, preferred_element_type=jnp.float32
            )

    leads = ((0, 1, LEADS[0]), (n_tm - 1, n_tm - 2, LEADS[1]))

    def keep_pace(count):
        for leader, follower, lead in leads:

            @pl.when((rank == leader) & (count >= lead) & (count < STEPS * SWEEPS))
            def _():
                pl.semaphore_signal(turn, inc=1, device_id={"tm": follower}, device_id_type=MESH)

            @pl.when((rank == follower) & (count + lead < STEPS * SWEEPS))
            def _():
                pl.semaphore_wait(turn, 1)

    def one_step(step, _):
        gp = lax.rem(step, 2)

        for sweep in range(SWEEPS):
            keep_pace(step * SWEEPS + sweep)

            def free(n, _):
                task(step, n // 4, n % 4, False)
                return 0

            lax.fori_loop(*FREE[sweep], free, 0)
            if sweep == 0:

                @pl.when(step == 0)
                def _():
                    all_of(*opening_refs).wait_recv()
                    for s in range(n_slice):
                        for part in range(slots // width):
                            held = opening_in[n_slice, pl.ds(part * width, width)]
                            held = jnp.broadcast_to(held[:, s * half:s * half + 1], (width, width))
                            hit = jnp.where(held == (lane + 1).astype(jnp.float32), 1.0, 0.0)
                            place[s, :, pl.ds(part * width, width)] = hit.T
                    couple(opening_in)

                @pl.when(step > 0)
                def _():
                    all_of(*gap_refs(gp)).wait_recv()
                    couple(landed.at[gp])

            if sweep == EARLY:
                @pl.when((rank == 0) & (step == STEPS - 1))
                def _():
                    by_component(0, n_comp, first)

            if sweep == SWEEPS - 1:
                @pl.when((rank == 0) & (step == STEPS - 1))
                def _():
                    by_component(0, n_comp - 1, second)

            def tied(s, _, sweep=sweep):
                task(step, sweep, n_free + s, True)
                return 0

            lax.fori_loop(0, n_slice, tied, 0)

        @pl.when(step < STEPS - 1)
        def _():
            later = 1 - gp

            @pl.when(step > 1)
            def _():
                all_of(*gap_refs(later)).wait_send()

            for s in range(n_slice):
                packed[later, s] = packed_rows(s, lax.rem((step + 1) * SWEEPS, 2))
            scatter(*gap_refs(later))

        @pl.when(step == 0)
        def _():
            coarse_coefficients()

        return 0

    lax.fori_loop(0, STEPS, one_step, 0)

    @pl.when(rank == n_tm - 1)
    def _():
        def one(c, _):
            pass_copy(v.at[end, place_of(n_slice - 1, c), pl.ds(1, planes), inner], c).start()
            return 0

        by_component(0, n_comp, one)

    @pl.when(rank > 0)
    def _():
        by_component(0, n_comp, first)

    by_component(jnp.where(rank == 0, n_comp - 1, 0), n_comp, second)

    @pl.when(rank < n_tm - 1)
    def _():
        def third(c, _):
            arrived(lambda way: delta_copy(1, c, way))
            coarse_before(1, c)
            for p in range(planes):
                passed[c, p] = coarse(1, c, p) + v[end, place_of(1, c), p + 1, inner]
            pass_copy(passed.at[c], c).start()
            return 0

        by_component(0, n_comp, third)

    for f in range(n_field):
        sent(lambda way: halo_copy(1 - end, f, way))
    sent(cond_copy)
    all_of(*opening_refs).wait_send()
    for gp in range(2):
        all_of(*gap_refs(gp)).wait_send()
    for c in range(n_comp):
        sent(lambda way: delta_copy(0, c, way))
        pass_copy(passed.at[c], c).wait_send()

        @pl.when(rank < n_tm - 1)
        def _():
            sent(lambda way: delta_copy(1, c, way))


def solution(mesh):
    n_space, n_tm = mesh.shape["space"], mesh.shape["tm"]

    def shards(states, sources, conductivity, gap_tile, gap_row):
        n_slice, n_comp, planes, rows, width = states.shape
        high = rows + 2 * PAD
        slots = n_space * CAP

        def f32(*shape):
            return pltpu.VMEM(shape, jnp.float32)

        def dma(*shape):
            return pltpu.SemaphoreType.DMA(shape)

        def body(*refs):
            kernel(n_space, n_tm, *refs)

        vmem = pl.BlockSpec(memory_space=pltpu.VMEM)
        return pl.pallas_call(
            body,
            out_shape=jax.ShapeDtypeStruct(states.shape, jnp.float32),
            in_specs=[pl.BlockSpec(memory_space=pl.ANY)] * 5,
            out_specs=vmem,
            scratch_shapes=[
                f32(2, n_slice * n_comp, planes + 2, high, width),
                f32(n_slice * n_comp, planes, rows, width),
                f32(n_slice * n_comp, planes, rows, width),
                f32(planes, rows, width),
                f32(planes, rows, width),
                f32(planes + 4, high, width),
                f32(planes + 2, high, width),
                f32(n_slice, n_comp, planes + 6, high, width),
                f32(planes + 4, rows, width),
                f32(planes + 4, rows, width),
                f32(planes + 4, rows, width),
                f32(n_slice, n_comp, planes, rows, width),
                f32(n_comp, planes, rows, width),
                f32(n_comp, planes, rows, width),
                pltpu.VMEM((n_slice, rows), jnp.int32),
                pltpu.VMEM((n_slice, rows), jnp.int32),
                f32(n_slice, slots, rows),
                f32(n_slice, rows, slots),
                f32(n_slice + 1, slots, width),
                f32(n_slice + 1, slots, width),
                f32(2, n_slice, slots, width),
                f32(2, n_slice, slots, width),
                f32(n_slice, rows, width),
                dma(4 + 2 * n_slice * n_comp), dma(2, n_slice * n_comp, 2), dma(2, n_slice * n_comp, 2),
                dma(3), dma(3), dma(2), dma(2),
                dma(n_slice, n_comp, 2), dma(n_slice, n_comp, 2), dma(n_comp), dma(n_comp),
                pltpu.SemaphoreType.REGULAR,
            ],
            compiler_params=pltpu.CompilerParams(
                collective_id=0, has_side_effects=True, vmem_limit_bytes=56 * 1024 * 1024
            ),
        )(states, sources, conductivity, gap_tile[:, :, 0], gap_row)

    return jax.shard_map(
        shards,
        mesh=mesh,
        in_specs=(
            P("tm", None, "space", None, None),
            P("tm", None, "space", None, None),
            P("space", None, None),
            P("tm", "space", None),
            P("tm", "space"),
        ),
        out_specs=P("tm", None, "space", None, None),
        check_vma=False,
    )
```

```python
import jax
import jax.numpy as jnp
from jax import lax
from jax.experimental import pallas as pl
from jax.experimental.pallas import tpu as pltpu
from jax.sharding import PartitionSpec as P

STEPS = 4
SWEEPS = 3
CAP = 8
PAD = 8

FREE = ((0, 6), (6, 9), (9, 12))
OPENING = (0, 1, 2, 3, 4, 5)
EARLY = 2
LEADS = (1, 4)

INVERSE_STEP = 2.0
GAP_GAIN = 1.0
MESH = pl.DeviceIdType.MESH
HIGHEST = lax.Precision.HIGHEST


def kernel(
    n_space, n_tm,
    states, sources, conduct, gap_tile, gap_row,
    out,
    v, rhs, sig, alpha, dinv, w1, w2, delta, cond8, gamma, dinv_c, start_state, new0, passed,
    tile_in, row_in, pick, place, opening, opening_in, packed, landed, coupled,
    load_sem, halo_send, halo_recv, gap_send, gap_recv,
    cond_send, cond_recv, delta_send, delta_recv, pass_send, pass_recv, turn,
):
    me = lax.axis_index("space")
    rank = lax.axis_index("tm")
    n_slice, n_comp, planes, rows, width = states.shape
    slots = n_space * CAP
    inner = pl.ds(PAD, rows)
    left_dev = {"space": jnp.maximum(me - 1, 0)}
    right_dev = {"space": jnp.minimum(me + 1, n_space - 1)}
    has_left = me > 0
    has_right = me < n_space - 1
    lane = lax.broadcasted_iota(jnp.int32, (rows, width), 1)
    sub = lax.broadcasted_iota(jnp.int32, (rows, width), 0)

    n_field = n_slice * n_comp
    n_free = n_field - n_slice

    def place_of(s, c):
        return jnp.where(c == 0, n_free + s, s * (n_comp - 1) + c - 1)

    barrier = pltpu.get_barrier_semaphore()

    def greet(i, _):
        peer = lax.rem(me + i, n_space)
        pl.semaphore_signal(barrier, inc=1, device_id={"space": peer}, device_id_type=MESH)
        return 0

    lax.fori_loop(1, n_space, greet, 0)
    next_rank = lax.rem(rank + 1, n_tm)
    for peer in (next_rank, lax.rem(rank + n_tm - 1, n_tm)):
        pl.semaphore_signal(barrier, inc=1, device_id={"tm": peer}, device_id_type=MESH)

    fields = [(s, c) for s in range(n_slice) for c in range(n_comp)]
    slot_of = {(s, c): n_free + s if c == 0 else s * (n_comp - 1) + c - 1 for s, c in fields}
    tile_load = pltpu.make_async_copy(gap_tile, tile_in, load_sem.at[0])
    row_load = pltpu.make_async_copy(gap_row, row_in, load_sem.at[1])
    cond_load = pltpu.make_async_copy(conduct, cond8.at[pl.ds(2, planes)], load_sem.at[2])
    state_load = pltpu.make_async_copy(states, start_state, load_sem.at[3])
    field_loads = {
        (s, c): pltpu.make_async_copy(
            states.at[s, c], v.at[0, slot_of[s, c], pl.ds(1, planes), inner], load_sem.at[4 + slot_of[s, c]]
        )
        for s, c in fields
    }
    source_loads = {
        (s, c): pltpu.make_async_copy(
            sources.at[s, c], sig.at[slot_of[s, c]], load_sem.at[4 + n_field + slot_of[s, c]]
        )
        for s, c in fields
    }
    tile_load.start()
    row_load.start()
    cond_load.start()
    for at in sorted(fields, key=lambda at: at[1]):
        field_loads[at].start()
    for at in fields:
        source_loads[at].start()
    state_load.start()

    edge_rows = jnp.zeros((PAD, width), jnp.float32)
    no_plane = jnp.zeros((rows, width), jnp.float32)

    def pad_planes(ref, index, count):
        for p in range(count):
            ref[index + (p, pl.ds(0, PAD))] = edge_rows
            ref[index + (p, pl.ds(PAD + rows, PAD))] = edge_rows

    def pad_fields(i, _):
        s, c = i // n_comp, i % n_comp
        f = place_of(s, c)
        for par in range(2):
            pad_planes(v, (par, f), planes + 2)
        pad_planes(delta, (s, c), planes + 6)
        return 0

    lax.fori_loop(0, n_slice * n_comp, pad_fields, 0)
    pad_planes(w1, (), planes + 4)
    pad_planes(w2, (), planes + 2)

    def clear(first, past):
        def one(i, _):
            s, c = i // n_comp, i % n_comp
            for par in range(2):
                v[par, i, 0 if first else planes + 1, inner] = no_plane
            for p in range(3):
                delta[s, c, p if first else planes + 3 + p, inner] = no_plane
            return 0

        lax.fori_loop(0, n_slice * n_comp, one, 0)
        for p in range(2):
            cond8[p if first else planes + 2 + p] = no_plane

    @pl.when(jnp.logical_not(has_left))
    def _():
        clear(True, 0)

    @pl.when(jnp.logical_not(has_right))
    def _():
        clear(False, 0)

    tile_load.wait()
    row_load.wait()
    names = []
    for s in range(n_slice):
        tile_row = jnp.broadcast_to(tile_in[s:s + 1].astype(jnp.float32), (rows, width))
        tile_col = tile_row.T
        before = jnp.where((tile_col == tile_row) & (sub < lane), 1.0, 0.0)
        position = jnp.sum(before, axis=0, keepdims=True)
        slot = tile_row[0:1] * CAP + position
        wide = lax.broadcasted_iota(jnp.int32, (slots, rows), 0).astype(jnp.float32)
        chosen = jnp.where(wide == slot, 1.0, 0.0)
        pick[s] = chosen
        target = row_in[s:s + 1].astype(jnp.float32) + 1.0
        named = jnp.sum(chosen * target, axis=1, keepdims=True)
        names.append(jnp.broadcast_to(named, (slots, width)))
    half = width // n_slice
    opening[n_slice] = jnp.where(lax.broadcasted_iota(jnp.int32, (slots, width), 1) < half, *names)

    def packed_rows(s, par):
        return jnp.dot(
            pick[s], v[par, n_free + s, 1, inner], precision=HIGHEST, preferred_element_type=jnp.float32
        )

    for at in fields:
        field_loads[at].wait()
    for s in range(n_slice):
        opening[s] = packed_rows(s, 0)

    def fine_coefficients():
        for p in range(planes):
            rate = INVERSE_STEP * cond8[p + 2]
            inverse = 1.0 / (rate + 6.0)
            dinv[p] = inverse
            alpha[p] = rate * inverse
        for at in fields:
            source_loads[at].wait()

        def scaled(f, _):
            for p in range(planes):
                sig[f, p] = sig[f, p] * dinv[p]
            return 0

        lax.fori_loop(0, n_field, scaled, 0)

    cond_load.wait()
    pl.semaphore_wait(barrier, n_space - 1 + 2)

    def halo_copy(par, f, way):
        return pltpu.make_async_remote_copy(
            src_ref=v.at[par, f, 1 if way == 0 else planes, inner],
            dst_ref=v.at[par, f, planes + 1 if way == 0 else 0, inner],
            send_sem=halo_send.at[par, f, way],
            recv_sem=halo_recv.at[par, f, way],
            device_id=left_dev if way == 0 else right_dev,
            device_id_type=MESH,
        )

    def delta_copy(s, c, way):
        return pltpu.make_async_remote_copy(
            src_ref=delta.at[s, c, pl.ds(3 if way == 0 else planes, 3), inner],
            dst_ref=delta.at[s, c, pl.ds(planes + 3 if way == 0 else 0, 3), inner],
            send_sem=delta_send.at[s, c, way],
            recv_sem=delta_recv.at[s, c, way],
            device_id=left_dev if way == 0 else right_dev,
            device_id_type=MESH,
        )

    def cond_copy(way):
        return pltpu.make_async_remote_copy(
            src_ref=cond8.at[pl.ds(2 if way == 0 else planes, 2)],
            dst_ref=cond8.at[pl.ds(planes + 2 if way == 0 else 0, 2)],
            send_sem=cond_send.at[way],
            recv_sem=cond_recv.at[way],
            device_id=left_dev if way == 0 else right_dev,
            device_id_type=MESH,
        )

    def start(copy):
        @pl.when(has_left)
        def _():
            copy(0).start()

        @pl.when(has_right)
        def _():
            copy(1).start()

    def arrived(copy):
        @pl.when(has_right)
        def _():
            copy(0).wait_recv()

        @pl.when(has_left)
        def _():
            copy(1).wait_recv()

    def sent(copy):
        @pl.when(has_left)
        def _():
            copy(0).wait_send()

        @pl.when(has_right)
        def _():
            copy(1).wait_send()

    def scatter(source, landing, send_sem, recv_sem):
        def one(i, _):
            peer = lax.rem(me + i, n_space)
            pltpu.make_async_remote_copy(
                src_ref=source.at[:, pl.ds(pl.multiple_of(peer * CAP, CAP), CAP)],
                dst_ref=landing.at[:, pl.ds(pl.multiple_of(me * CAP, CAP), CAP)],
                send_sem=send_sem,
                recv_sem=recv_sem,
                device_id={"space": peer},
                device_id_type=MESH,
            ).start()
            return 0

        lax.fori_loop(1, n_space, one, 0)
        own = pl.ds(pl.multiple_of(me * CAP, CAP), CAP)
        for s in range(source.shape[0]):
            landing[s, own] = source[s, own]

    def all_of(source, landing, send_sem, recv_sem):
        most = pl.ds(0, (n_space - 1) * CAP)
        return pltpu.make_async_remote_copy(
            src_ref=source.at[:, most],
            dst_ref=landing.at[:, most],
            send_sem=send_sem,
            recv_sem=recv_sem,
            device_id=left_dev,
            device_id_type=MESH,
        )

    def gap_refs(gp):
        return packed.at[gp], landed.at[gp], gap_send.at[gp], gap_recv.at[gp]

    for f in OPENING:
        start(lambda way: halo_copy(0, f, way))
    opening_refs = (opening, opening_in, gap_send.at[2], gap_recv.at[2])
    scatter(*opening_refs)
    start(cond_copy)
    fine_coefficients()

    def beside(ref, index, p):
        here = ref[index + (p, inner)]
        total = ref[index + (p - 1, inner)] + ref[index + (p + 1, inner)]
        total = total + ref[index + (p, pl.ds(PAD - 1, rows))] + ref[index + (p, pl.ds(PAD + 1, rows))]
        total = total + jnp.where(lane == 0, 0.0, pltpu.roll(here, 1, 1))
        total = total + jnp.where(lane == width - 1, 0.0, pltpu.roll(here, width - 1, 1))
        return total, here

    def task(step, sweep, f, tied):
        count = step * SWEEPS + sweep
        par = lax.rem(count, 2)
        onto = 1 - par

        @pl.when(sweep == 0)
        def _():
            for p in range(planes):
                base = alpha[p] * v[par, f, p + 1, inner] + sig[f, p]
                if tied and p == 0:
                    base = base + dinv[0] * coupled[f - n_free]
                rhs[f, p] = base

        arrived(lambda way: halo_copy(par, f, way))

        @pl.when(count > 0)
        def _():
            sent(lambda way: halo_copy(onto, f, way))

        def plane(p):
            total, _ = beside(v, (par, f), p)
            v[onto, f, p, inner] = rhs[f, p - 1] + dinv[p - 1] * total

        plane(1)
        plane(planes)

        @pl.when((step < STEPS - 1) | (sweep < SWEEPS - 1))
        def _():
            start(lambda way: halo_copy(onto, f, way))

        for p in range(2, planes):
            plane(p)

    def coarse_coefficients():
        arrived(cond_copy)
        for p in range(planes + 4):
            rate = INVERSE_STEP * cond8[p] / STEPS
            inverse = 1.0 / (rate + 6.0)
            if p < 2:
                inverse = jnp.where(has_left, inverse, 0.0)
            if p >= planes + 2:
                inverse = jnp.where(has_right, inverse, 0.0)
            dinv_c[p] = inverse
            gamma[p] = rate * inverse

    state_load.wait()
    end = (STEPS * SWEEPS) % 2

    def pass_copy(source, c):
        return pltpu.make_async_remote_copy(
            src_ref=source,
            dst_ref=new0.at[c],
            send_sem=pass_send.at[c],
            recv_sem=pass_recv.at[c],
            device_id={"tm": next_rank},
            device_id_type=MESH,
        )

    def first(c, _):
        pass_copy(new0.at[c], c).wait_recv()
        for p in range(planes):
            delta[0, c, p + 3, inner] = new0[c, p] - start_state[0, c, p]
        start(lambda way: delta_copy(0, c, way))
        for p in range(planes):
            out[0, c, p] = new0[c, p]
        return 0

    def coarse(s, c, p):
        total, _ = beside(w2, (), p + 1)
        return gamma[p + 2] * delta[s, c, p + 3, inner] + dinv_c[p + 2] * total

    def coarse_before(s, c):
        for p in range(planes + 4):
            total, here = beside(delta, (s, c), p + 1)
            w1[p, inner] = gamma[p] * here + dinv_c[p] * total
        for p in range(planes + 2):
            total, _ = beside(w1, (), p + 1)
            w2[p, inner] = gamma[p + 1] * delta[s, c, p + 2, inner] + dinv_c[p + 1] * total

    def second(c, _):
        arrived(lambda way: delta_copy(0, c, way))
        coarse_before(0, c)
        for p in range(planes):
            value = coarse(0, c, p) + v[end, place_of(0, c), p + 1, inner]
            out[1, c, p] = value
            delta[1, c, p + 3, inner] = value - start_state[1, c, p]

        @pl.when(rank < n_tm - 1)
        def _():
            start(lambda way: delta_copy(1, c, way))

        return 0

    def by_component(first_at, past, act):
        def one(i, _):
            return act(lax.rem(i + 1, n_comp), 0)

        lax.fori_loop(first_at, past, one, 0)

    def couple(landing):
        for s in range(n_slice):
            coupled[s] = GAP_GAIN * jnp.dot(
                place[s], landing[s], precision=HIGHEST, preferred_element_type=jnp.float32
            )

    leads = ((0, 1, LEADS[0]), (n_tm - 1, n_tm - 2, LEADS[1]))

    def keep_pace(count):
        for leader, follower, lead in leads:

            @pl.when((rank == leader) & (count >= lead) & (count < STEPS * SWEEPS))
            def _():
                pl.semaphore_signal(turn, inc=1, device_id={"tm": follower}, device_id_type=MESH)

            @pl.when((rank == follower) & (count + lead < STEPS * SWEEPS))
            def _():
                pl.semaphore_wait(turn, 1)

    def one_step(step, _):
        gp = lax.rem(step, 2)

        for sweep in range(SWEEPS):
            keep_pace(step * SWEEPS + sweep)

            def free(n, _):
                task(step, n // 4, n % 4, False)
                return 0

            lax.fori_loop(*FREE[sweep], free, 0)
            if sweep == 0:

                @pl.when(step == 0)
                def _():
                    all_of(*opening_refs).wait_recv()
                    for s in range(n_slice):
                        for part in range(slots // width):
                            held = opening_in[n_slice, pl.ds(part * width, width)]
                            held = jnp.broadcast_to(held[:, s * half:s * half + 1], (width, width))
                            hit = jnp.where(held == (lane + 1).astype(jnp.float32), 1.0, 0.0)
                            place[s, :, pl.ds(part * width, width)] = hit.T
                    couple(opening_in)

                @pl.when(step > 0)
                def _():
                    all_of(*gap_refs(gp)).wait_recv()
                    couple(landed.at[gp])

            if sweep == EARLY:
                @pl.when((rank == 0) & (step == STEPS - 1))
                def _():
                    by_component(0, n_comp, first)

            if sweep == SWEEPS - 1:
                @pl.when((rank == 0) & (step == STEPS - 1))
                def _():
                    by_component(0, n_comp - 1, second)

            def tied(s, _, sweep=sweep):
                task(step, sweep, n_free + s, True)
                return 0

            lax.fori_loop(0, n_slice, tied, 0)

        @pl.when(step < STEPS - 1)
        def _():
            later = 1 - gp

            @pl.when(step > 1)
            def _():
                all_of(*gap_refs(later)).wait_send()

            for s in range(n_slice):
                packed[later, s] = packed_rows(s, lax.rem((step + 1) * SWEEPS, 2))
            scatter(*gap_refs(later))

        @pl.when(step == 0)
        def _():
            coarse_coefficients()

        return 0

    lax.fori_loop(0, STEPS, one_step, 0)

    @pl.when(rank == n_tm - 1)
    def _():
        def one(c, _):
            pass_copy(v.at[end, place_of(n_slice - 1, c), pl.ds(1, planes), inner], c).start()
            return 0

        by_component(0, n_comp, one)

    @pl.when(rank > 0)
    def _():
        by_component(0, n_comp, first)

    by_component(jnp.where(rank == 0, n_comp - 1, 0), n_comp, second)

    @pl.when(rank < n_tm - 1)
    def _():
        def third(c, _):
            arrived(lambda way: delta_copy(1, c, way))
            coarse_before(1, c)
            for p in range(planes):
                passed[c, p] = coarse(1, c, p) + v[end, place_of(1, c), p + 1, inner]
            pass_copy(passed.at[c], c).start()
            return 0

        by_component(0, n_comp, third)

    for f in range(n_field):
        sent(lambda way: halo_copy(1 - end, f, way))
    sent(cond_copy)
    all_of(*opening_refs).wait_send()
    for gp in range(2):
        all_of(*gap_refs(gp)).wait_send()
    for c in range(n_comp):
        sent(lambda way: delta_copy(0, c, way))
        pass_copy(passed.at[c], c).wait_send()

        @pl.when(rank < n_tm - 1)
        def _():
            sent(lambda way: delta_copy(1, c, way))


def solution(mesh):
    n_space, n_tm = mesh.shape["space"], mesh.shape["tm"]

    def shards(states, sources, conductivity, gap_tile, gap_row):
        n_slice, n_comp, planes, rows, width = states.shape
        high = rows + 2 * PAD
        slots = n_space * CAP

        def f32(*shape):
            return pltpu.VMEM(shape, jnp.float32)

        def dma(*shape):
            return pltpu.SemaphoreType.DMA(shape)

        def body(*refs):
            kernel(n_space, n_tm, *refs)

        vmem = pl.BlockSpec(memory_space=pltpu.VMEM)
        return pl.pallas_call(
            body,
            out_shape=jax.ShapeDtypeStruct(states.shape, jnp.float32),
            in_specs=[pl.BlockSpec(memory_space=pl.ANY)] * 5,
            out_specs=vmem,
            scratch_shapes=[
                f32(2, n_slice * n_comp, planes + 2, high, width),
                f32(n_slice * n_comp, planes, rows, width),
                f32(n_slice * n_comp, planes, rows, width),
                f32(planes, rows, width),
                f32(planes, rows, width),
                f32(planes + 4, high, width),
                f32(planes + 2, high, width),
                f32(n_slice, n_comp, planes + 6, high, width),
                f32(planes + 4, rows, width),
                f32(planes + 4, rows, width),
                f32(planes + 4, rows, width),
                f32(n_slice, n_comp, planes, rows, width),
                f32(n_comp, planes, rows, width),
                f32(n_comp, planes, rows, width),
                pltpu.VMEM((n_slice, rows), jnp.int32),
                pltpu.VMEM((n_slice, rows), jnp.int32),
                f32(n_slice, slots, rows),
                f32(n_slice, rows, slots),
                f32(n_slice + 1, slots, width),
                f32(n_slice + 1, slots, width),
                f32(2, n_slice, slots, width),
                f32(2, n_slice, slots, width),
                f32(n_slice, rows, width),
                dma(4 + 2 * n_slice * n_comp), dma(2, n_slice * n_comp, 2), dma(2, n_slice * n_comp, 2),
                dma(3), dma(3), dma(2), dma(2),
                dma(n_slice, n_comp, 2), dma(n_slice, n_comp, 2), dma(n_comp), dma(n_comp),
                pltpu.SemaphoreType.REGULAR,
            ],
            compiler_params=pltpu.CompilerParams(
                collective_id=0, has_side_effects=True, vmem_limit_bytes=56 * 1024 * 1024
            ),
        )(states, sources, conductivity, gap_tile[:, :, 0], gap_row)

    return jax.shard_map(
        shards,
        mesh=mesh,
        in_specs=(
            P("tm", None, "space", None, None),
            P("tm", None, "space", None, None),
            P("space", None, None),
            P("tm", "space", None),
            P("tm", "space"),
        ),
        out_specs=P("tm", None, "space", None, None),
        check_vma=False,
    )
```
